256 devices in a mesh: patch: 32 (over z_lo, y, core), tensor: 8 (over z_hi, x).
Axes of the slice: x: 4, y: 4, z: 8 (z_hi: 2, z_lo: 4; z = z_hi * 4 + z_lo), core: 2. Of those that a mesh axis runs over, the one named last changes fastest.
Arguments:
- latent: float32 [4608, 3072], P('patch'), may hold values from -6 to 6
- timesteps: int32 [3], replicated, may hold values from 0 to 7, as said below
- sigmas: float32 [8], replicated, may hold values from 0 to 1, as said below
- mod_table: float32 [8, 3, 3072], replicated, may hold values from -3 to 3
- w_in: bfloat16 [3072, 12288], P('patch', 'tensor'), may hold values from -1.7320508 to 1.7320508
- w_out: bfloat16 [8192, 3072], P('tensor', 'patch'), may hold values from -0.0625 to 0.0625
- q_gain: float32 [128], replicated, may hold values from 0.5 to 5
- k_gain: float32 [128], replicated, may hold values from 0.5 to 5
- stale_keys: bfloat16 [4608, 2048], P('patch', 'tensor'), may hold values from -60 to 60
- stale_values: bfloat16 [4608, 2048], P('patch', 'tensor'), may hold values from -6 to 6
Outputs:
- velocity: float32 [4608, 3072], P('patch')
- current: float32 [4608, 3072], P('patch')
The draws below stay inside these ranges and needn't reach their ends.
Inputs may be any that keep to these rules, and one draw needn't show every extreme that they name: `timesteps`: strictly falling, from 7 to 0. `sigmas`: rising with the index, the last entry 1.
All inputs are finite; a program needn't handle non-finite values.
Results may differ from the reference program's by a relative error of at most 0.02.
Values may be sent and summed in bfloat16 or wider, within the bound.
No kernel may reach another device: no remote copies, remote signals or barrier semaphores. Data moves between devices by JAX's collectives and lax.ppermute only.
A program may use at most 128 MiB of HBM per device.

```python
import math
import jax
import jax.numpy as jnp
from jax import lax

D = 3072
HEADS = 16
HEAD_DIM = 128
MLP = 6144
TOK_DEV = 144
STEPS = 2
TIMES = 8
GRID = 64
INNER = 2048
TOKENS = 4608
TEXT = 512
N_PATCH = 32
N_TENSOR = 8


def loud_layout(key):
    key = jax.random.fold_in(key, 101)
    pair_ranks = jax.random.permutation(jax.random.fold_in(key, 1), HEAD_DIM // 2)
    loud_pairs = pair_ranks < max(1, HEAD_DIM // 32)
    loud_dims = jnp.repeat(loud_pairs, 2)
    head_ranks = jax.random.permutation(jax.random.fold_in(key, 2), HEADS)
    tied_heads = head_ranks < max(1, HEADS // 4)
    return (loud_dims, tied_heads)


def key_gain(key, loud_dims, bounds):
    key = jax.random.fold_in(key, 103)
    quiet_gain = jax.random.uniform(jax.random.fold_in(key, 1), (HEAD_DIM,), jnp.float32, bounds[0], bounds[1])
    loud_gain = jax.random.uniform(jax.random.fold_in(key, 2), (HEAD_DIM,), jnp.float32, bounds[2], bounds[3])
    return jnp.where(loud_dims, loud_gain, quiet_gain)


def input_weights(key, loud_dims, tied_heads, loud_scale):
    inner_local = INNER // N_TENSOR
    heads_local = HEADS // N_TENSOR
    width_in = 3 * inner_local + MLP // N_TENSOR
    raw_cols = jnp.clip(jax.random.normal(key, (D, N_TENSOR, width_in), jnp.float32), -6.0, 6.0)
    query_cols = raw_cols[:, :, :inner_local].reshape(D, N_TENSOR, heads_local, HEAD_DIM)
    key_cols = raw_cols[:, :, inner_local:2 * inner_local].reshape(D, N_TENSOR, heads_local, HEAD_DIM)
    head_tied = tied_heads.reshape(N_TENSOR, heads_local)[None, :, :, None]
    key_cols = jnp.where(head_tied, key_cols, key_cols)
    lifted = jnp.where(head_tied, jnp.where(loud_dims, loud_scale, 1.0), 1.0)
    query_cols = (query_cols * lifted).reshape(D, N_TENSOR, inner_local)
    key_cols = (key_cols * lifted).reshape(D, N_TENSOR, inner_local)
    joined = jnp.concatenate([query_cols, key_cols, raw_cols[:, :, 2 * inner_local:]], axis=2)
    return (joined.reshape(D, 3 * INNER + MLP) / math.sqrt(D)).astype(jnp.bfloat16)


def key_rows(key, loud_dims, tied_heads, loud_scale, gain_vec):
    raw_rows = jnp.clip(jax.random.normal(key, (TOKENS, HEADS, HEAD_DIM), jnp.float32), -3.0, 3.0)
    lifted = jnp.where(loud_dims, loud_scale, 1.0)
    amplitude = jnp.where(tied_heads[:, None], lifted[None, :], 1.0)
    return (raw_rows * amplitude[None] * gain_vec).reshape(TOKENS, INNER).astype(jnp.bfloat16)


def draw_timesteps(key, part):
    key = jax.random.fold_in(key, 13)
    order = jax.random.permutation(key, TIMES - 2).astype(jnp.int32)
    middle, unused = lax_top(order[:STEPS - 1])
    first = jnp.full((1,), TIMES - 1, jnp.int32)
    last = jnp.zeros((1,), jnp.int32)
    return jnp.concatenate([first, middle + 1, last]).astype(jnp.int32)


def lax_top(values):
    return jax.lax.top_k(values, values.shape[0])


def draw_sigmas(key, part):
    key = jax.random.fold_in(key, 17)
    spread = jax.random.uniform(key, (TIMES,), jnp.float32, 0.0, 1.0)
    gaps = jnp.exp(spread * math.log(6.0))
    rising = jnp.cumsum(gaps) / jnp.sum(gaps)
    return jnp.minimum(rising, 1.0)


def draw_w_in(key, part):
    loud_dims, tied_heads = loud_layout(key)
    key = jax.random.fold_in(key, 7)
    return input_weights(key, loud_dims, tied_heads, 1.0)


def draw_q_gain(key, part):
    loud_dims, tied_heads = loud_layout(key)
    key = jax.random.fold_in(key, 5)
    bounds = (0.5, 2.5, 0.5, 2.5)
    quiet_gain = jax.random.uniform(jax.random.fold_in(key, 1), (HEAD_DIM,), jnp.float32, bounds[0], bounds[1])
    loud_gain = jax.random.uniform(jax.random.fold_in(key, 2), (HEAD_DIM,), jnp.float32, bounds[2], bounds[3])
    return jnp.where(loud_dims, loud_gain, quiet_gain)


def draw_k_gain(key, part):
    loud_dims, tied_heads = loud_layout(key)
    return key_gain(key, loud_dims, (0.5, 2.5, 0.5, 2.5))


def draw_stale_keys(key, part):
    loud_dims, tied_heads = loud_layout(key)
    gain_vec = key_gain(key, loud_dims, (0.5, 2.5, 0.5, 2.5))
    loud_scale = 1.0
    key = jax.random.fold_in(key, 11)
    return key_rows(key, loud_dims, tied_heads, loud_scale, gain_vec)


def shard_levels(own_key, dims, shards, smallest, largest):
    factor_of, own = 1.0, jax.random.fold_in(own_key, 6)
    for position, shards_of in shards:
        heights = jnp.exp(jax.random.uniform(jax.random.fold_in(own, position), (shards_of,), jnp.float32, smallest / len(shards), largest / len(shards)))
        factor_of = factor_of * jnp.repeat(heights, dims[position] // shards_of).reshape([-1 if axis == position else 1 for axis in range(len(dims))])
    return factor_of


def gaussian(stream_key, extent, deviation, bound, pieces=(), held_as=jnp.bfloat16):
    array = deviation * jax.random.normal(stream_key, extent, jnp.float32)
    if pieces:
        array = array * shard_levels(stream_key, extent, pieces, -0.22, 0.18)
    return jnp.clip(array, -bound, bound).astype(held_as)


def setup_inputs(seed: int = 0) -> dict:
    keys = jax.random.split(jax.random.key(seed), 11)
    return {
        "latent": gaussian(keys[0], (TOKENS, D), 1.0, 6.0, ((0, 32),), jnp.float32),
        "timesteps": draw_timesteps(jax.random.fold_in(keys[10], 71), 0),
        "sigmas": draw_sigmas(jax.random.fold_in(keys[10], 71), 0),
        "mod_table": gaussian(keys[3], (TIMES, 3, D), 0.5, 3.0, (), jnp.float32),
        "w_in": draw_w_in(jax.random.fold_in(keys[10], 71), 0),
        "w_out": gaussian(keys[5], (INNER + MLP, D), (INNER + MLP) ** -0.5, 0.0625, ((0, 8), (1, 32))),
        "q_gain": draw_q_gain(jax.random.fold_in(keys[10], 71), 0),
        "k_gain": draw_k_gain(jax.random.fold_in(keys[10], 71), 0),
        "stale_keys": draw_stale_keys(jax.random.fold_in(keys[10], 71), 0),
        "stale_values": gaussian(keys[9], (TOKENS, INNER), 1.0, 6.0, ((0, 32), (1, 8))),
    }


epsilon = 1e-06

def frequencies(width_axis):
    return 1.0 / jnp.power(10000.0, jnp.arange(0, width_axis, 2, dtype=jnp.float32) / width_axis)

def rope_tables(token_index, text_count, grid_width, head_dim):
    first_width = head_dim // 8
    other_width = (head_dim - first_width) // 2
    image_index = jnp.maximum(token_index - text_count, 0)
    image_token = token_index >= text_count
    grid_row = jnp.where(image_token, image_index // grid_width, 0).astype(jnp.float32)
    grid_column = jnp.where(image_token, image_index % grid_width, 0).astype(jnp.float32)
    angles = jnp.concatenate([jnp.zeros_like(grid_row)[:, None] * frequencies(first_width)[None, :], grid_row[:, None] * frequencies(other_width)[None, :], grid_column[:, None] * frequencies(other_width)[None, :]], axis=1)
    paired = jnp.repeat(angles, 2, axis=1)
    parity = jnp.arange(head_dim, dtype=jnp.int32) % 2
    sign_pattern = jnp.where(parity == 0, -1.0, 1.0)
    return (jnp.cos(paired), jnp.sin(paired) * sign_pattern)

def rotate(shaped, cosine_table, sine_table):
    parity = jnp.arange(shaped.shape[-1], dtype=jnp.int32) % 2
    swapped = jnp.where(parity == 0, jnp.roll(shaped, -1, axis=-1), jnp.roll(shaped, 1, axis=-1))
    return shaped * cosine_table[:, None, :] + swapped * sine_table[:, None, :]

def layer_norm_mod(hidden, shift, scale_vec):
    mean_val = lax.optimization_barrier(jnp.mean(hidden, -1, keepdims=True))
    centred = hidden - mean_val
    variance = lax.optimization_barrier(jnp.mean(centred * centred, -1, keepdims=True))
    return (centred * lax.rsqrt(variance + epsilon) * (1.0 + scale_vec) + shift).astype(jnp.bfloat16)

def head_norm(columns, gain_vec, head_count, cosine_table, sine_table):
    shaped = columns.reshape(columns.shape[0], head_count, -1)
    scaled = shaped * lax.rsqrt(lax.optimization_barrier(jnp.mean(shaped * shaped, -1, keepdims=True)) + epsilon) * gain_vec
    return rotate(scaled, cosine_table, sine_table).astype(jnp.bfloat16)

def reference(latent, timesteps, sigmas, mod_table, w_in, w_out, q_gain, k_gain, stale_keys, stale_values):
    inner_local = INNER // N_TENSOR
    width_in = 3 * inner_local + MLP // N_TENSOR
    score_scale = 1.0 / HEAD_DIM ** 0.5
    cosine_table, sine_table = rope_tables(jnp.arange(TOKENS, dtype=jnp.int32), TEXT, GRID, HEAD_DIM)
    current = latent
    keys_old = stale_keys.reshape(TOKENS, HEADS, HEAD_DIM)
    values_old = stale_values.reshape(TOKENS, HEADS, HEAD_DIM)
    velocity = latent
    for denoise in range(STEPS):
        modulation = jnp.take(mod_table, timesteps[denoise], axis=0)
        step_size = jnp.take(sigmas, timesteps[denoise + 1]) - jnp.take(sigmas, timesteps[denoise])
        normed = layer_norm_mod(current, modulation[0], modulation[1])
        projected = jnp.dot(normed, w_in, preferred_element_type=jnp.float32).reshape(TOKENS, N_TENSOR, width_in)
        queries = head_norm(projected[:, :, :inner_local].reshape(TOKENS, INNER), q_gain, HEADS, cosine_table, sine_table)
        fresh_keys = head_norm(projected[:, :, inner_local:2 * inner_local].reshape(TOKENS, INNER), k_gain, HEADS, cosine_table, sine_table)
        fresh_values = projected[:, :, 2 * inner_local:3 * inner_local].reshape(TOKENS, HEADS, HEAD_DIM).astype(jnp.bfloat16)
        activated = jax.nn.gelu(projected[:, :, 3 * inner_local:], approximate=True).astype(jnp.bfloat16)

        def one_patch(patch_index):
            row_begin = (patch_index * TOK_DEV).astype(jnp.int32)
            query_rows = lax.dynamic_slice_in_dim(queries, row_begin, TOK_DEV, 0)
            key_all = lax.dynamic_update_slice_in_dim(keys_old, lax.dynamic_slice_in_dim(fresh_keys, row_begin, TOK_DEV, 0), row_begin, 0)
            value_all = lax.dynamic_update_slice_in_dim(values_old, lax.dynamic_slice_in_dim(fresh_values, row_begin, TOK_DEV, 0), row_begin, 0)
            scores = jnp.einsum('qhd,khd->hqk', query_rows.astype(jnp.float32), key_all.astype(jnp.float32)) * score_scale
            row_top = lax.optimization_barrier(jnp.max(scores, -1, keepdims=True))
            exponent = jnp.exp(scores - row_top)
            row_total = lax.optimization_barrier(jnp.sum(exponent, -1))
            mixed_out = jnp.einsum('hqk,khd->hqd', exponent.astype(jnp.bfloat16).astype(jnp.float32), value_all.astype(jnp.float32)) / row_total[..., None]
            return jnp.transpose(mixed_out, (1, 0, 2)).astype(jnp.bfloat16)
        attended = lax.map(one_patch, jnp.arange(N_PATCH, dtype=jnp.int32)).reshape(TOKENS, N_TENSOR, inner_local)
        joined = jnp.concatenate([attended, activated], axis=2).reshape(TOKENS, -1)
        branch = jnp.dot(joined, w_out, preferred_element_type=jnp.float32)
        velocity = current + modulation[2] * branch
        current = current + step_size * velocity
        keys_old = fresh_keys
        values_old = fresh_values
    return (velocity, current)
```

```python
import jax
import jax.numpy as jnp
from jax import lax
from jax.sharding import PartitionSpec as P

STEPS = 2
GRID = 64
epsilon = 1e-06

NZ, NY, NC, NH, NX = 4, 4, 2, 2, 4
AXES = ("patch", "tensor")


def flat(zl, y, c, zh, x):
    return (((zl * NY + y) * NC + c) * NH + zh) * NX + x


def pairs(move):
    out = []
    for zl in range(NZ):
        for y in range(NY):
            for c in range(NC):
                for zh in range(NH):
                    for x in range(NX):
                        out.append((flat(zl, y, c, zh, x), flat(*move(zl, y, c, zh, x))))
    return out


def from_z(a, k):
    return lax.ppermute(a, AXES, pairs(lambda zl, y, c, zh, x: ((zl - k) % NZ, y, c, zh, x)))


def from_y(a, k):
    return lax.ppermute(a, AXES, pairs(lambda zl, y, c, zh, x: (zl, (y - k) % NY, c, zh, x)))


def from_x(a, k):
    return lax.ppermute(a, AXES, pairs(lambda zl, y, c, zh, x: (zl, y, c, zh, (x - k) % NX)))


def swap_core(a):
    return lax.ppermute(a, AXES, pairs(lambda zl, y, c, zh, x: (zl, y, 1 - c, zh, x)))


def swap_zh(a):
    return lax.ppermute(a, AXES, pairs(lambda zl, y, c, zh, x: (zl, y, c, 1 - zh, x)))


def frequencies(width_axis):
    return 1.0 / jnp.power(10000.0, jnp.arange(0, width_axis, 2, dtype=jnp.float32) / width_axis)


def rope_tables(token_index, text_count, grid_width, head_dim):
    first_width = head_dim // 8
    other_width = (head_dim - first_width) // 2
    image_index = jnp.maximum(token_index - text_count, 0)
    image_token = token_index >= text_count
    grid_row = jnp.where(image_token, image_index // grid_width, 0).astype(jnp.float32)
    grid_column = jnp.where(image_token, image_index % grid_width, 0).astype(jnp.float32)
    angles = jnp.concatenate(
        [
            jnp.zeros_like(grid_row)[:, None] * frequencies(first_width)[None, :],
            grid_row[:, None] * frequencies(other_width)[None, :],
            grid_column[:, None] * frequencies(other_width)[None, :],
        ],
        axis=1,
    )
    paired = jnp.repeat(angles, 2, axis=1)
    parity = jnp.arange(head_dim, dtype=jnp.int32) % 2
    sign_pattern = jnp.where(parity == 0, -1.0, 1.0)
    return (jnp.cos(paired), jnp.sin(paired) * sign_pattern)


def head_norm(columns, gain_vec, cosine_table, sine_table):
    scaled = columns * lax.rsqrt(jnp.mean(columns * columns, -1, keepdims=True) + epsilon) * gain_vec
    parity = jnp.arange(columns.shape[-1], dtype=jnp.int32) % 2
    swapped = jnp.where(parity == 0, jnp.roll(scaled, -1, axis=-1), jnp.roll(scaled, 1, axis=-1))
    return (scaled * cosine_table + swapped * sine_table).astype(jnp.bfloat16)


def layer_norm_mod(hidden, shift, scale_vec):
    mean_val = jnp.mean(hidden, -1, keepdims=True)
    centred = hidden - mean_val
    variance = jnp.mean(centred * centred, -1, keepdims=True)
    return (centred * lax.rsqrt(variance + epsilon) * (1.0 + scale_vec) + shift).astype(
        jnp.bfloat16
    )


def pick_entry(table, wanted):
    positions = jnp.arange(table.shape[0], dtype=jnp.int32)
    chosen = positions == wanted
    return jnp.sum(jnp.where(chosen.reshape((-1,) + (1,) * (table.ndim - 1)), table, 0.0), 0)


def gather_z(block, start):
    rows = block.shape[0]
    whole = jnp.zeros((NZ, rows, block.shape[1]), block.dtype)
    whole = lax.dynamic_update_index_in_dim(whole, block, start, 0)
    for k in range(1, NZ):
        piece = from_z(block, k)
        whole = lax.dynamic_update_index_in_dim(whole, piece, (start + k) % NZ, 0)
    return whole.reshape(NZ * rows, block.shape[1])


def gather_y(block):
    half = block.shape[0] // 2
    after = from_y(block, 1)
    before = from_y(block, NY - 1)
    low = from_y(before[:half], NY - 1)
    high = from_y(after[half:], 1)
    return [block, after, jnp.concatenate([low, high], 0), before]


def attend(queries, fresh_keys, fresh_values, key_slots, value_slots):
    rows, head_dim = queries.shape
    own = rows // 2
    keys = jnp.concatenate([fresh_keys] + key_slots, 0)
    values = jnp.concatenate([fresh_values] + value_slots, 0)
    scores = jnp.dot(queries, keys.T, preferred_element_type=jnp.float32) / head_dim**0.5
    col = jnp.arange(keys.shape[0], dtype=jnp.int32)[None, :]
    patch_of_row = (jnp.arange(rows, dtype=jnp.int32) // own)[:, None]
    patch_of_col = (col % rows) // own
    fresh = col < rows
    ours = col < 2 * rows
    drop = ours & ((patch_of_row == patch_of_col) != fresh)
    scores = jnp.where(drop, -1e30, scores)
    row_top = jnp.max(scores, -1, keepdims=True)
    exponent = jnp.exp(scores - row_top)
    row_total = jnp.sum(exponent, -1, keepdims=True)
    weighted = jnp.dot(exponent.astype(jnp.bfloat16), values, preferred_element_type=jnp.float32)
    return (weighted / row_total).astype(jnp.bfloat16)


def local(
    latent, timesteps, sigmas, mod_table, w_in, w_out, q_gain, k_gain, stale_keys, stale_values
):
    own_rows, width = latent.shape
    head_dim = q_gain.shape[0]
    patch = lax.axis_index("patch")
    c = patch % NC
    y = (patch // NC) % NY
    zl = patch // (NC * NY)
    x = lax.axis_index("tensor") % NX
    first = c == 0
    block = width // NY
    piece = block // NZ
    text_count = own_rows * lax.axis_size("patch") // 9

    def keep_and_send(for_core_0, for_core_1):
        return jnp.where(first, for_core_0, for_core_1), jnp.where(first, for_core_1, for_core_0)

    def share(for_core_0, for_core_1):
        keep, send = keep_and_send(for_core_0, for_core_1)
        other = swap_core(send)
        return jnp.where(
            first, jnp.concatenate([keep, other], 0), jnp.concatenate([other, keep], 0)
        )

    def share_own_first(array):
        half = array.shape[1] // 2
        keep, send = keep_and_send(array[:, :half], array[:, half:])
        return jnp.concatenate([keep, swap_core(send)], 0)

    inner = 2 * head_dim
    hidden = (w_in.shape[1] - 3 * inner) // 2

    def qkv_columns(j):
        return jnp.concatenate(
            [w_in[:, i * inner + j * head_dim : i * inner + (j + 1) * head_dim] for i in range(3)], 1
        )

    def mlp_columns(j):
        return w_in[:, 3 * inner + j * hidden : 3 * inner + (j + 1) * hidden]

    out_t = w_out.T

    def out_columns(j):
        return jnp.concatenate(
            [
                out_t[:, j * head_dim : (j + 1) * head_dim],
                out_t[:, inner + j * hidden : inner + (j + 1) * hidden],
            ],
            1,
        )

    qkv_slots = gather_y(gather_z(share(qkv_columns(0), qkv_columns(1)), zl))
    mlp_slots = gather_y(gather_z(share(mlp_columns(0), mlp_columns(1)), zl))
    out_slots = gather_y(gather_z(share(out_columns(0), out_columns(1)), zl))

    def gather_old(keys, values):
        rows = keys.shape[0]
        both = jnp.concatenate([keys, values], 1)
        line = [both] + [from_z(both, k) for k in range(1, NZ)]
        slots = gather_y(jnp.concatenate(line, 0))
        return [s[:, :head_dim] for s in slots], [s[:, head_dim:] for s in slots]

    keys_old = share_own_first(stale_keys)
    values_old = share_own_first(stale_values)

    own_index = jnp.arange(own_rows, dtype=jnp.int32)
    token_index = jnp.concatenate(
        [patch * own_rows + own_index, (patch + 1 - 2 * c) * own_rows + own_index]
    )
    cosine_table, sine_table = rope_tables(token_index, text_count, GRID, head_dim)
    current = latent
    velocity = latent

    for denoise in range(STEPS):
        modulation = pick_entry(mod_table, timesteps[denoise])
        step_size = pick_entry(sigmas, timesteps[denoise + 1]) - pick_entry(
            sigmas, timesteps[denoise]
        )
        key_slots, value_slots = gather_old(keys_old, values_old)
        normed = layer_norm_mod(current, modulation[0], modulation[1])
        normed = jnp.concatenate([normed, swap_core(normed)], 0)
        rows = normed.shape[0]
        by_y = normed.reshape(rows, NZ, NY, piece).transpose(2, 0, 1, 3).reshape(NY, rows, block)
        mine = [lax.dynamic_index_in_dim(by_y, (y + k) % NY, 0, keepdims=False) for k in range(NY)]
        qkv = sum(
            jnp.dot(mine[k], qkv_slots[k], preferred_element_type=jnp.float32) for k in range(NY)
        )
        mlp = sum(
            jnp.dot(mine[k], mlp_slots[k], preferred_element_type=jnp.float32) for k in range(NY)
        )
        queries = head_norm(qkv[:, :head_dim], q_gain, cosine_table, sine_table)
        fresh_keys = head_norm(qkv[:, head_dim : 2 * head_dim], k_gain, cosine_table, sine_table)
        fresh_values = qkv[:, 2 * head_dim :].astype(jnp.bfloat16)
        activated = jax.nn.gelu(mlp, approximate=True).astype(jnp.bfloat16)
        attended = attend(queries, fresh_keys, fresh_values, key_slots, value_slots)
        joined = jnp.concatenate([attended, activated], 1)

        parts = []
        for k in range(NY):
            part = jnp.dot(joined, out_slots[k].T, preferred_element_type=jnp.float32)
            other = swap_core(part[own_rows:].astype(jnp.bfloat16))
            parts.append((part[:own_rows] + other.astype(jnp.float32)).astype(jnp.bfloat16))
        stacked = jnp.stack(parts, 0)
        total = lax.dynamic_index_in_dim(stacked, x, 0, keepdims=False).astype(jnp.float32)
        for k in range(1, NX):
            send = lax.dynamic_index_in_dim(stacked, (x + k) % NX, 0, keepdims=False)
            total = total + from_x(send, NX - k).astype(jnp.float32)
        half_sum = total.astype(jnp.bfloat16)
        total = half_sum.astype(jnp.float32) + swap_zh(half_sum).astype(jnp.float32)
        done = total.astype(jnp.bfloat16)
        whole = jnp.zeros((NY, own_rows, block), jnp.bfloat16)
        whole = lax.dynamic_update_index_in_dim(whole, done, (y + x) % NY, 0)
        for k in range(1, NX):
            whole = lax.dynamic_update_index_in_dim(whole, from_x(done, k), (y + x + k) % NY, 0)
        branch = (
            whole.reshape(NY, own_rows, NZ, piece)
            .transpose(1, 2, 0, 3)
            .reshape(own_rows, width)
            .astype(jnp.float32)
        )
        velocity = current + modulation[2] * branch
        current = current + step_size * velocity
        keys_old = fresh_keys
        values_old = fresh_values
    return (velocity, current)


def solution(mesh):
    return jax.shard_map(
        local,
        mesh=mesh,
        in_specs=(
            P("patch", None),
            P(),
            P(),
            P(),
            P("patch", "tensor"),
            P("tensor", "patch"),
            P(),
            P(),
            P("patch", "tensor"),
            P("patch", "tensor"),
        ),
        out_specs=(P("patch", None), P("patch", None)),
        check_vma=False,
    )
```

```python
import functools

import jax
import numpy as np
import jax.numpy as jnp
from jax import lax
from jax.experimental import pallas as pl
from jax.experimental.pallas import tpu as pltpu
from jax.sharding import PartitionSpec as P

STEPS = 2
GRID = 64
epsilon = 1e-06

VMEM = pl.BlockSpec(memory_space=pltpu.VMEM)
SMEM = pl.BlockSpec(memory_space=pltpu.SMEM)
ANY = pl.BlockSpec(memory_space=pl.ANY)
PARAMS = pltpu.CompilerParams(vmem_limit_bytes=40 * 1024 * 1024)

NZ, NY, NC, NH, NX = 4, 4, 2, 2, 4
AXES = ("patch", "tensor")


def flat(zl, y, c, zh, x):
    return (((zl * NY + y) * NC + c) * NH + zh) * NX + x


def pairs(move):
    out = []
    for zl in range(NZ):
        for y in range(NY):
            for c in range(NC):
                for zh in range(NH):
                    for x in range(NX):
                        out.append((flat(zl, y, c, zh, x), flat(*move(zl, y, c, zh, x))))
    return out


def from_z(a, k):
    return lax.ppermute(a, AXES, pairs(lambda zl, y, c, zh, x: ((zl - k) % NZ, y, c, zh, x)))


def from_y(a, k):
    return lax.ppermute(a, AXES, pairs(lambda zl, y, c, zh, x: (zl, (y - k) % NY, c, zh, x)))


def swap_y(a):
    return lax.ppermute(a, AXES, pairs(lambda zl, y, c, zh, x: (zl, y ^ 1, c, zh, x)))


def flip_y(a):
    return lax.ppermute(a, AXES, pairs(lambda zl, y, c, zh, x: (zl, NY - 1 - y, c, zh, x)))


def from_x(a, k):
    return lax.ppermute(a, AXES, pairs(lambda zl, y, c, zh, x: (zl, y, c, zh, (x - k) % NX)))


def swap_core(a):
    return lax.ppermute(a, AXES, pairs(lambda zl, y, c, zh, x: (zl, y, 1 - c, zh, x)))


def swap_zh(a):
    return lax.ppermute(a, AXES, pairs(lambda zl, y, c, zh, x: (zl, y, c, 1 - zh, x)))


def frequencies(width_axis):
    return 1.0 / np.power(10000.0, np.arange(0, width_axis, 2) / width_axis)


def rope_rates(head_dim):
    first_width = head_dim // 8
    other_width = (head_dim - first_width) // 2
    none, rates = np.zeros(first_width // 2), frequencies(other_width)
    by_row = np.concatenate([none, rates, 0 * rates])
    by_column = np.concatenate([none, 0 * rates, rates])
    return np.repeat(np.stack([by_row, by_column]), 2, axis=1).astype(np.float32)


def rope_kernel(place_ref, rates_ref, cos_ref, sin_ref, *, text_count):
    rows, head_dim = cos_ref.shape
    half = rows // 2
    patch, other = place_ref[0], place_ref[1]
    index = lax.broadcasted_iota(jnp.int32, (rows, head_dim), 0)
    token = jnp.where(index < half, patch * half + index, other * half + index - half)
    image = jnp.maximum(token - text_count, 0)
    row = (image // GRID).astype(jnp.float32)
    column = (image % GRID).astype(jnp.float32)
    angles = row * rates_ref[0:1, :] + column * rates_ref[1:2, :]
    parity = lax.broadcasted_iota(jnp.int32, (rows, head_dim), 1) % 2
    cos_ref[...] = jnp.cos(angles)
    sin_ref[...] = jnp.sin(angles) * jnp.where(parity == 0, -1.0, 1.0)


def rope_tables(patch, other, rows, head_dim, text_count):
    return pl.pallas_call(
        functools.partial(rope_kernel, text_count=text_count),
        out_shape=[jax.ShapeDtypeStruct((rows, head_dim), jnp.float32)] * 2,
        in_specs=[SMEM, VMEM],
        out_specs=[VMEM] * 2,
        compiler_params=PARAMS,
    )(jnp.stack([patch, other]), jnp.asarray(rope_rates(head_dim)))


def layer_norm_mod(hidden, shift, scale_vec):
    mean_val = jnp.mean(hidden, -1, keepdims=True)
    centred = hidden - mean_val
    variance = jnp.mean(centred * centred, -1, keepdims=True)
    return (centred * lax.rsqrt(variance + epsilon) * (1.0 + scale_vec) + shift).astype(
        jnp.bfloat16
    )


def pick_entry(table, wanted):
    positions = jnp.arange(table.shape[0], dtype=jnp.int32)
    chosen = positions == wanted
    return jnp.sum(jnp.where(chosen.reshape((-1,) + (1,) * (table.ndim - 1)), table, 0.0), 0)


def after(array, done):
    return lax.optimization_barrier((array, done))[0]


def line_pieces(block):
    return [block] + [from_z(block, k) for k in range(1, NZ)]


def line_of(block):
    return jnp.concatenate(line_pieces(block), 0)


def pack(array):
    rows = array.shape[0] // 3
    return jnp.concatenate([array[i * rows : (i + 1) * rows] for i in range(3)], 1)


class Spread:
    def __init__(self, line, ahead, behind, ahead_half, behind_half):
        self.rows, self.columns = line[0].shape
        self.arrays = line + [s[0] for s in (ahead, behind, ahead_half, behind_half)]
        ahead, behind, ahead_half, behind_half = (
            s[1] for s in (ahead, behind, ahead_half, behind_half)
        )
        self.places = [(kz, 0, kz, 0) for kz in range(NZ)]
        self.places += [(NZ, ahead + kz * self.rows, kz, 1) for kz in range(NZ)]
        self.places += [(NZ + 1, behind + kz * self.rows, kz, NY - 1) for kz in range(NZ)]
        for kz in range(NZ):
            late = kz >= NZ // 2
            at = (ahead_half if late else behind_half) + kz % (NZ // 2) * self.rows
            self.places.append((NZ + 2 if late else NZ + 3, at, kz, 2))


def arrange(places, refs, held, zl, y):
    rows = held.shape[1]
    for n, at, kz, ky in places:
        chip = lax.rem(zl + kz, NZ) * NY + lax.rem(y + ky, NY)
        held[chip] = refs[n][at : at + rows, :]


def turn(columns, gain, cosine, sine):
    scaled = (
        columns
        * lax.rsqrt(jnp.mean(columns * columns, axis=-1, keepdims=True) + epsilon)
        * gain
    )
    width = columns.shape[1]
    parity = lax.broadcasted_iota(jnp.int32, columns.shape, 1) % 2
    swapped = jnp.where(
        parity == 0, pltpu.roll(scaled, width - 1, 1), pltpu.roll(scaled, 1, 1)
    )
    return (scaled * cosine + swapped * sine).astype(jnp.bfloat16)


def arranged(spread):
    return jax.ShapeDtypeStruct((NZ * NY, spread.rows, spread.columns), jnp.bfloat16)


def projected(places, place_ref, own_ref, other_ref, w_refs, held):
    if places is None:
        held = w_refs[0]
    else:
        arrange(places, w_refs, held, place_ref[0], place_ref[1])
    normed = jnp.concatenate([own_ref[...], other_ref[...]], 0)
    w = held[...].reshape(normed.shape[1], held.shape[2])
    return jnp.dot(normed, w, preferred_element_type=jnp.float32)


def qkv_kernel(
    place_ref, own_ref, other_ref, qg_ref, kg_ref, cos_ref, sin_ref, *refs, places
):
    w_refs, held = (refs[:-2], None) if places is None else (refs[:-3], refs[-1])
    q_ref, fresh_ref = refs[len(w_refs) : len(w_refs) + 2]
    head_dim = q_ref.shape[1]
    qkv = projected(places, place_ref, own_ref, other_ref, w_refs, held)
    cosine, sine = cos_ref[...], sin_ref[...]
    q_ref[...] = turn(qkv[:, :head_dim], qg_ref[...], cosine, sine)
    fresh_ref[:, :head_dim] = turn(qkv[:, head_dim : 2 * head_dim], kg_ref[...], cosine, sine)
    fresh_ref[:, head_dim:] = qkv[:, 2 * head_dim :].astype(jnp.bfloat16)


def sources(w):
    if isinstance(w, Spread):
        return w.arrays, w.places, [arranged(w)]
    return [w], None, []


def project_cost(rows):
    size = 3072 * 384
    return pl.CostEstimate(flops=2 * rows * size, bytes_accessed=2 * size, transcendentals=0)


def project_qkv(place, own, other, w, q_gain, k_gain, cosine, sine):
    rows, head_dim = cosine.shape
    arrays, places, held = sources(w)
    outs = pl.pallas_call(
        functools.partial(qkv_kernel, places=places),
        out_shape=[
            jax.ShapeDtypeStruct((rows, head_dim), jnp.bfloat16),
            jax.ShapeDtypeStruct((rows, 2 * head_dim), jnp.bfloat16),
        ]
        + held,
        in_specs=[SMEM] + [VMEM] * (6 + len(arrays)),
        out_specs=[VMEM] * (2 + len(held)),
        compiler_params=PARAMS,
        cost_estimate=project_cost(rows),
    )(place, own, other, q_gain[None, :], k_gain[None, :], cosine, sine, *arrays)
    return outs[0], outs[1], outs[2] if held else w


def mlp_kernel(place_ref, own_ref, other_ref, *refs, places):
    w_refs, held = (refs[:-1], None) if places is None else (refs[:-2], refs[-1])
    hidden = projected(places, place_ref, own_ref, other_ref, w_refs, held)
    refs[len(w_refs)][...] = jax.nn.gelu(hidden, approximate=True).astype(jnp.bfloat16)


def project_mlp(place, own, other, w):
    rows = 2 * own.shape[0]
    arrays, places, held = sources(w)
    outs = pl.pallas_call(
        functools.partial(mlp_kernel, places=places),
        out_shape=[jax.ShapeDtypeStruct((rows, arrays[0].shape[-1]), jnp.bfloat16)] + held,
        in_specs=[SMEM] + [VMEM] * (2 + len(arrays)),
        out_specs=[VMEM] * (1 + len(held)),
        compiler_params=PARAMS,
        cost_estimate=project_cost(rows),
    )(place, own, other, *arrays)
    return outs[0], outs[1] if held else w


def unpack(packed):
    third = packed.shape[-1] // 3
    return jnp.concatenate([packed[:, i * third : (i + 1) * third] for i in range(3)], 0)


def mix_kernel(place_ref, q_ref, fresh_ref, act_ref, *refs, back_places, old_places, sizes):
    backs, olds, back_rows = sizes
    back_refs, old_refs, refs = refs[:backs], refs[backs : backs + olds], refs[backs + olds :]
    own_refs, other_refs, refs = refs[:NX], refs[NX : 2 * NX], refs[2 * NX :]
    scores_ref = refs[-1]
    rows, head_dim = q_ref.shape
    half = rows // 2
    zl, y, x = place_ref[0], place_ref[1], place_ref[2]
    first_key = back_rows + back_rows // 3
    if back_places is None:
        back_ref = back_refs[0]
    else:
        back_ref = refs[0]
        arrange(back_places, back_refs, back_ref, zl, y)
    q = q_ref[...]
    scale = 1.0 / head_dim**0.5
    dims = (((1,), (1,)), ((), ()))
    row_patch = lax.broadcasted_iota(jnp.int32, (rows, rows), 0) // half
    col_patch = lax.broadcasted_iota(jnp.int32, (rows, rows), 1) // half
    same = row_patch == col_patch

    beside = y + 1 - 2 * lax.rem(y, 2)
    order = [y, beside, NY - 1 - y, NY - 1 - beside]

    def old_keys(n):
        if old_places is None:
            chip = lax.rem(zl + n // NY, NZ) * NY + order[n % NY]
            return unpack(back_ref[chip, first_key:, :])
        i, at, _, _ = old_places[n]
        return old_refs[i][at : at + rows, :head_dim]

    def old_values(n):
        if old_places is None:
            at = n % NY * rows
            return old_refs[n // NY][at : at + rows, :]
        i, at, _, _ = old_places[n]
        return old_refs[i][at : at + rows, head_dim:]

    first = jnp.where(
        same,
        lax.dot_general(q, fresh_ref[:, :head_dim], dims, preferred_element_type=jnp.float32)
        * scale,
        -1e30,
    )
    scores_ref[0] = first
    top = jnp.max(first, axis=1, keepdims=True)
    chips = NZ * NY
    for n in range(chips):
        s = (
            lax.dot_general(q, old_keys(n), dims, preferred_element_type=jnp.float32)
            * scale
        )
        if n == 0:
            s = jnp.where(same, -1e30, s)
        scores_ref[n + 1] = s
        top = jnp.maximum(top, jnp.max(s, axis=1, keepdims=True))
    total = jnp.zeros((rows, 1), jnp.float32)
    mixed = jnp.zeros((rows, head_dim), jnp.float32)
    for n in range(chips + 1):
        e = jnp.exp(scores_ref[n] - top)
        total = total + jnp.sum(e, axis=1, keepdims=True)
        mixed = mixed + jnp.dot(
            e.astype(jnp.bfloat16),
            old_values(n - 1) if n else fresh_ref[:, head_dim:],
            preferred_element_type=jnp.float32,
        )
    attended = (mixed / total).astype(jnp.bfloat16)
    activated = act_ref[...]
    for k in range(NX):
        at = lax.rem(x + k, NX) * NY
        w_mlp = back_ref[pl.ds(at, NY), :back_rows, :].reshape(NY * back_rows, -1)
        w_att = jnp.concatenate(
            [unpack(back_ref[at + j, back_rows:first_key, :]) for j in range(NY)], 0
        )
        part = lax.dot_general(activated, w_mlp, dims, preferred_element_type=jnp.float32)
        part = part + lax.dot_general(
            attended, w_att, dims, preferred_element_type=jnp.float32
        )
        own_refs[k][...] = part[:half]
        other_refs[k][...] = part[half:].astype(jnp.bfloat16)


def mix(place, queries, fresh, activated, back, back_rows, old):
    rows, head_dim = queries.shape
    half = rows // 2
    chips = NZ * NY
    block = NY * back_rows
    back_arrays, back_places, held = sources(back)
    old_arrays, old_places = (old.arrays, old.places) if isinstance(old, Spread) else (old, None)
    kinds = [jnp.float32] * NX + [jnp.bfloat16] * NX
    outs = pl.pallas_call(
        functools.partial(
            mix_kernel,
            back_places=back_places,
            old_places=old_places,
            sizes=(len(back_arrays), len(old_arrays), back_rows),
        ),
        out_shape=[jax.ShapeDtypeStruct((half, block), kind) for kind in kinds] + held,
        in_specs=[SMEM] + [VMEM] * (3 + len(back_arrays) + len(old_arrays)),
        out_specs=[VMEM] * (len(kinds) + len(held)),
        scratch_shapes=[pltpu.VMEM((chips + 1, rows, rows), jnp.float32)],
        compiler_params=PARAMS,
        cost_estimate=pl.CostEstimate(
            flops=4 * rows * rows * chips * head_dim + 8 * rows * block * 4 * head_dim,
            bytes_accessed=12 * 1024 * 1024,
            transcendentals=rows * rows * chips,
        ),
    )(place, queries, fresh, activated, *back_arrays, *old_arrays)
    return outs[:NX], outs[NX : 2 * NX], outs[2 * NX] if held else back


def update_kernel(place_ref, step_ref, cur_ref, mod_ref, *refs, last):
    pieces, refs = refs[:NX], refs[NX:]
    out_a, out_b, branch_ref = refs
    block = pieces[0].shape[1]
    for k in range(NX):
        at = pl.multiple_of(lax.rem(place_ref[2] + k, NX) * block, block)
        branch_ref[:, pl.ds(at, block)] = pieces[k][...].astype(jnp.float32)
    current = cur_ref[...]
    velocity = current + mod_ref[0:1, :] * branch_ref[...]
    current = current + step_ref[0] * velocity
    if last:
        out_a[...] = velocity
        out_b[...] = current
    else:
        out_a[...] = current
        centred = current - jnp.mean(current, axis=-1, keepdims=True)
        variance = jnp.mean(centred * centred, axis=-1, keepdims=True)
        out_b[...] = (
            centred * lax.rsqrt(variance + epsilon) * (1.0 + mod_ref[1:2, :]) + mod_ref[2:3, :]
        ).astype(jnp.bfloat16)


def update(place, step_size, current, mods, pieces, last):
    rows, width = current.shape
    tile = rows // 3
    block = width // NX
    whole = pl.BlockSpec((tile, width), lambda i: (i, 0))
    return pl.pallas_call(
        functools.partial(update_kernel, last=last),
        out_shape=[
            jax.ShapeDtypeStruct(current.shape, jnp.float32),
            jax.ShapeDtypeStruct(current.shape, jnp.float32 if last else jnp.bfloat16),
        ],
        grid=(rows // tile,),
        in_specs=[SMEM, SMEM, whole, pl.BlockSpec(mods.shape, lambda i: (0, 0))]
        + [pl.BlockSpec((tile, block), lambda i: (i, 0))] * NX,
        out_specs=[whole] * 2,
        scratch_shapes=[pltpu.VMEM((tile, width), jnp.float32)],
        compiler_params=PARAMS,
        cost_estimate=pl.CostEstimate(
            flops=20 * current.size, bytes_accessed=14 * current.size, transcendentals=0
        ),
    )(place, step_size, current, mods, *pieces)


def local(
    latent, timesteps, sigmas, mod_table, w_in, w_out, q_gain, k_gain, stale_keys, stale_values
):
    own_rows, width = latent.shape
    head_dim = q_gain.shape[0]
    patch = lax.axis_index("patch")
    c = patch % NC
    y = (patch // NC) % NY
    zl = patch // (NC * NY)
    x = lax.axis_index("tensor") % NX
    first = c == 0
    block = width // NY
    text_count = own_rows * lax.axis_size("patch") // 9

    def keep_and_send(for_core_0, for_core_1):
        return jnp.where(first, for_core_0, for_core_1), jnp.where(first, for_core_1, for_core_0)

    def in_core_order(keep, other):
        return jnp.where(
            first, jnp.concatenate([keep, other], 0), jnp.concatenate([other, keep], 0)
        )

    inner = 2 * head_dim
    hidden = (w_in.shape[1] - 3 * inner) // 2

    def qkv_columns(j):
        return jnp.concatenate(
            [w_in[:, i * inner + j * head_dim : i * inner + (j + 1) * head_dim] for i in range(3)], 1
        )

    def mlp_columns(j):
        return w_in[:, 3 * inner + j * hidden : 3 * inner + (j + 1) * hidden]

    def out_columns(j):
        return jnp.concatenate(
            [
                out_t[:, j * head_dim : (j + 1) * head_dim],
                out_t[:, inner + j * hidden : inner + (j + 1) * hidden],
            ],
            1,
        )

    def old_columns(j):
        return jnp.concatenate(
            [a[:, j * head_dim : (j + 1) * head_dim] for a in (stale_keys, stale_values)], 1
        )

    place = jnp.stack([zl, y, x])
    cat = functools.partial(jnp.concatenate, axis=0)

    keep, send = keep_and_send(qkv_columns(0), qkv_columns(1))
    other = swap_core(send)
    qkv_line = line_pieces(in_core_order(keep, other))
    keep, send = keep_and_send(old_columns(0), old_columns(1))
    old = cat([keep, swap_core(send)])
    old_values = old[:, head_dim:]
    old_values = cat([old_values, swap_y(old_values)])
    w_in, latent, mod_table = after((w_in, latent, mod_table), qkv_line[1])
    keep, send = keep_and_send(mlp_columns(0), mlp_columns(1))
    mlp_block = in_core_order(keep, swap_core(send))
    old_values = cat([old_values, flip_y(after(old_values, mlp_block))])
    mods = [pick_entry(mod_table, timesteps[s]) for s in range(STEPS)]
    steps = [
        (
            pick_entry(sigmas, timesteps[s + 1]) - pick_entry(sigmas, timesteps[s])
        ).reshape(1)
        for s in range(STEPS)
    ]
    first_normed = layer_norm_mod(latent, mods[0][0], mods[0][1])
    normed = first_normed, swap_core(first_normed)

    qkv_message = cat(qkv_line)
    qkv_message, mlp_block = after((qkv_message, mlp_block), (old_values, normed))
    q_rows = qkv_message.shape[0] // 2
    ahead_1, behind_1 = from_y(qkv_message, 1), from_y(qkv_message, NY - 1)
    mlp_line = line_pieces(mlp_block)
    w_out, patch = after((w_out, patch), mlp_line[1])
    out_t = w_out.T
    back_rows = 2 * out_t.shape[0]
    cosine_table, sine_table = rope_tables(
        patch, patch + 1 - 2 * c, 2 * own_rows, head_dim, text_count
    )
    keep, send = keep_and_send(out_columns(0), out_columns(1))
    out_block = in_core_order(keep, swap_core(send))
    back_block = cat(
        [out_block[:, head_dim:], pack(out_block[:, :head_dim]), pack(old[:, :head_dim])]
    )

    mlp_message = cat(mlp_line)
    mlp_message, ahead_1, behind_1, back_block = after(
        (mlp_message, ahead_1, behind_1, back_block), (cosine_table, sine_table)
    )
    ahead_2, behind_2 = from_y(mlp_message, 1), from_y(mlp_message, NY - 1)
    back_line = line_pieces(after(back_block, (ahead_1, behind_1, mlp_message)))
    ahead_1h = from_y(after(ahead_1[q_rows:], back_line[1]), 1)
    behind_1h = from_y(after(behind_1[:q_rows], ahead_2), NY - 1)

    back_message = cat(back_line)
    back_message, old_values, ahead_2, behind_2 = after(
        (back_message, old_values, ahead_2, behind_2), (ahead_1h, behind_1h)
    )
    ahead_3, behind_3 = from_y(back_message, 1), from_y(back_message, NY - 1)
    old_values = line_pieces(after(old_values, (ahead_2, behind_2, back_message)))
    ahead_2h = from_y(after(ahead_2[q_rows:], old_values[1]), 1)
    behind_2h = from_y(after(behind_2[:q_rows], old_values[3]), NY - 1)
    w_qkv = Spread(qkv_line, (ahead_1, 0), (behind_1, 0), (ahead_1h, 0), (behind_1h, 0))
    w_mlp = Spread(mlp_line, (ahead_2, 0), (behind_2, 0), (ahead_2h, 0), (behind_2h, 0))

    def wave_4(fresh):
        ahead, behind, fresh = after(
            (ahead_3, behind_3, fresh), (fresh, old_values, ahead_2h, behind_2h)
        )
        half = NZ // 2 * back_block.shape[0]
        ahead_3h = from_y(ahead[half:], 1)
        behind_3h = from_y(behind[:half], NY - 1)
        back = Spread(back_line, (ahead, 0), (behind, 0), (ahead_3h, 0), (behind_3h, 0))
        return back, line_pieces(after(fresh, (ahead, behind)))

    current = latent
    old = old_values

    for denoise in range(STEPS):
        last = denoise + 1 == STEPS
        queries, fresh, w_qkv = project_qkv(
            place, *normed, w_qkv, q_gain, k_gain, cosine_table, sine_table
        )
        if not last:
            w_back, new_line = wave_4(fresh)
            new_message = cat(new_line)
            new_ahead, new_behind = from_y(new_message, 1), from_y(new_message, NY - 1)
        activated, w_mlp = project_mlp(place, *normed, w_mlp)
        own, other, w_back = mix(place, queries, fresh, activated, w_back, back_rows, old)
        blocks = [
            (own[k] + swap_core(other[k]).astype(jnp.float32)).astype(jnp.bfloat16)
            for k in range(NX)
        ]
        total = blocks[0].astype(jnp.float32)
        for k in [2, 1, 3]:
            total = total + from_x(blocks[k], NX - k).astype(jnp.float32)
        half_sum = total.astype(jnp.bfloat16)
        total = half_sum.astype(jnp.float32) + swap_zh(half_sum).astype(jnp.float32)
        done = total.astype(jnp.bfloat16)
        if not last:
            done, new_ahead, new_behind = after((done, new_ahead, new_behind), done)
            half = new_message.shape[0] // 2
            new_halves = from_y(new_ahead[half:], 1), from_y(new_behind[:half], NY - 1)
            old = Spread(
                new_line,
                (new_ahead, 0),
                (new_behind, 0),
                (new_halves[0], 0),
                (new_halves[1], 0),
            )
        pieces = [done] + [from_x(done, k) for k in range(1, NX)]
        gate = mods[denoise][2]
        if not last:
            after_mods = jnp.stack([gate, mods[denoise + 1][1], mods[denoise + 1][0]])
            current, normed = update(place, steps[denoise], current, after_mods, pieces, last)
            normed = normed, swap_core(normed)
        else:
            return update(place, steps[denoise], current, gate[None, :], pieces, last)


def solution(mesh):
    return jax.shard_map(
        local,
        mesh=mesh,
        in_specs=(
            P("patch", None),
            P(),
            P(),
            P(),
            P("patch", "tensor"),
            P("tensor", "patch"),
            P(),
            P(),
            P("patch", "tensor"),
            P("patch", "tensor"),
        ),
        out_specs=(P("patch", None), P("patch", None)),
        check_vma=False,
    )
```

```python
import functools

import jax
import numpy as np
import jax.numpy as jnp
from jax import lax
from jax.experimental import pallas as pl
from jax.experimental.pallas import tpu as pltpu
from jax.sharding import PartitionSpec as P

STEPS = 2
GRID = 64
epsilon = 1e-06

VMEM = pl.BlockSpec(memory_space=pltpu.VMEM)
SMEM = pl.BlockSpec(memory_space=pltpu.SMEM)
ANY = pl.BlockSpec(memory_space=pl.ANY)
PARAMS = pltpu.CompilerParams(vmem_limit_bytes=40 * 1024 * 1024)

NZ, NY, NC, NH, NX = 4, 4, 2, 2, 4
AXES = ("patch", "tensor")


def flat(zl, y, c, zh, x):
    return (((zl * NY + y) * NC + c) * NH + zh) * NX + x


def pairs(move):
    out = []
    for zl in range(NZ):
        for y in range(NY):
            for c in range(NC):
                for zh in range(NH):
                    for x in range(NX):
                        out.append((flat(zl, y, c, zh, x), flat(*move(zl, y, c, zh, x))))
    return out


def from_z(a, k):
    return lax.ppermute(a, AXES, pairs(lambda zl, y, c, zh, x: ((zl - k) % NZ, y, c, zh, x)))


def from_y(a, k):
    return lax.ppermute(a, AXES, pairs(lambda zl, y, c, zh, x: (zl, (y - k) % NY, c, zh, x)))


def swap_y(a):
    return lax.ppermute(a, AXES, pairs(lambda zl, y, c, zh, x: (zl, y ^ 1, c, zh, x)))


def flip_y(a):
    return lax.ppermute(a, AXES, pairs(lambda zl, y, c, zh, x: (zl, NY - 1 - y, c, zh, x)))


def from_x(a, k):
    return lax.ppermute(a, AXES, pairs(lambda zl, y, c, zh, x: (zl, y, c, zh, (x - k) % NX)))


def swap_core(a):
    return lax.ppermute(a, AXES, pairs(lambda zl, y, c, zh, x: (zl, y, 1 - c, zh, x)))


def swap_zh(a):
    return lax.ppermute(a, AXES, pairs(lambda zl, y, c, zh, x: (zl, y, c, 1 - zh, x)))


def frequencies(width_axis):
    return 1.0 / np.power(10000.0, np.arange(0, width_axis, 2) / width_axis)


def rope_rates(head_dim):
    first_width = head_dim // 8
    other_width = (head_dim - first_width) // 2
    none, rates = np.zeros(first_width // 2), frequencies(other_width)
    by_row = np.concatenate([none, rates, 0 * rates])
    by_column = np.concatenate([none, 0 * rates, rates])
    return np.repeat(np.stack([by_row, by_column]), 2, axis=1).astype(np.float32)


def rope_kernel(place_ref, rates_ref, cos_ref, sin_ref, *, text_count):
    rows, head_dim = cos_ref.shape
    half = rows // 2
    patch, other = place_ref[0], place_ref[1]
    index = lax.broadcasted_iota(jnp.int32, (rows, head_dim), 0)
    token = jnp.where(index < half, patch * half + index, other * half + index - half)
    image = jnp.maximum(token - text_count, 0)
    row = (image // GRID).astype(jnp.float32)
    column = (image % GRID).astype(jnp.float32)
    angles = row * rates_ref[0:1, :] + column * rates_ref[1:2, :]
    parity = lax.broadcasted_iota(jnp.int32, (rows, head_dim), 1) % 2
    cos_ref[...] = jnp.cos(angles)
    sin_ref[...] = jnp.sin(angles) * jnp.where(parity == 0, -1.0, 1.0)


def rope_tables(patch, other, rows, head_dim, text_count):
    return pl.pallas_call(
        functools.partial(rope_kernel, text_count=text_count),
        out_shape=[jax.ShapeDtypeStruct((rows, head_dim), jnp.float32)] * 2,
        in_specs=[SMEM, VMEM],
        out_specs=[VMEM] * 2,
        compiler_params=PARAMS,
    )(jnp.stack([patch, other]), jnp.asarray(rope_rates(head_dim)))


def after(array, done):
    return lax.optimization_barrier((array, done))[0]


def line_pieces(block):
    return [block] + [from_z(block, k) for k in range(1, NZ)]


def line_of(block):
    return jnp.concatenate(line_pieces(block), 0)


def pack(array):
    rows = array.shape[0] // 3
    return jnp.concatenate([array[i * rows : (i + 1) * rows] for i in range(3)], 1)


class Spread:
    def __init__(self, line, ahead, behind, ahead_half, behind_half):
        self.rows, self.columns = line[0].shape
        self.arrays = line + [s[0] for s in (ahead, behind, ahead_half, behind_half)]
        ahead, behind, ahead_half, behind_half = (
            s[1] for s in (ahead, behind, ahead_half, behind_half)
        )
        self.places = [(kz, 0, kz, 0) for kz in range(NZ)]
        self.places += [(NZ, ahead + kz * self.rows, kz, 1) for kz in range(NZ)]
        self.places += [(NZ + 1, behind + kz * self.rows, kz, NY - 1) for kz in range(NZ)]
        for kz in range(NZ):
            late = kz >= NZ // 2
            at = (ahead_half if late else behind_half) + kz % (NZ // 2) * self.rows
            self.places.append((NZ + 2 if late else NZ + 3, at, kz, 2))


def arrange(places, refs, held, zl, y):
    rows = held.shape[1]
    for n, at, kz, ky in places:
        chip = lax.rem(zl + kz, NZ) * NY + lax.rem(y + ky, NY)
        held[chip] = refs[n][at : at + rows, :]


def turn(columns, gain, cosine, sine):
    scaled = (
        columns
        * lax.rsqrt(jnp.mean(columns * columns, axis=-1, keepdims=True) + epsilon)
        * gain
    )
    width = columns.shape[1]
    parity = lax.broadcasted_iota(jnp.int32, columns.shape, 1) % 2
    swapped = jnp.where(
        parity == 0, pltpu.roll(scaled, width - 1, 1), pltpu.roll(scaled, 1, 1)
    )
    return (scaled * cosine + swapped * sine).astype(jnp.bfloat16)


def arranged(spread):
    return jax.ShapeDtypeStruct((NZ * NY, spread.rows, spread.columns), jnp.bfloat16)


def projected(places, place_ref, own_ref, other_ref, w_refs, held):
    if places is None:
        held = w_refs[0]
    else:
        arrange(places, w_refs, held, place_ref[0], place_ref[1])
    normed = jnp.concatenate([own_ref[...], other_ref[...]], 0)
    rows = normed.shape[1] // held.shape[0]
    w = held[:, :rows, :].reshape(normed.shape[1], held.shape[2])
    return jnp.dot(normed, w, preferred_element_type=jnp.float32)


def qkv_kernel(
    place_ref, own_ref, other_ref, qg_ref, kg_ref, cos_ref, sin_ref, *refs, places
):
    w_refs, held = (refs[:-2], None) if places is None else (refs[:-3], refs[-1])
    q_ref, fresh_ref = refs[len(w_refs) : len(w_refs) + 2]
    head_dim = q_ref.shape[1]
    qkv = projected(places, place_ref, own_ref, other_ref, w_refs, held)
    cosine, sine = cos_ref[...], sin_ref[...]
    q_ref[...] = turn(qkv[:, :head_dim], qg_ref[...], cosine, sine)
    fresh_ref[:, :head_dim] = turn(qkv[:, head_dim : 2 * head_dim], kg_ref[...], cosine, sine)
    fresh_ref[:, head_dim:] = qkv[:, 2 * head_dim :].astype(jnp.bfloat16)


def sources(w):
    if isinstance(w, Spread):
        return w.arrays, w.places, [arranged(w)]
    return [w], None, []


def project_cost(rows):
    size = 3072 * 384
    return pl.CostEstimate(flops=2 * rows * size, bytes_accessed=2 * size, transcendentals=0)


def project_qkv(place, own, other, w, q_gain, k_gain, cosine, sine):
    rows, head_dim = cosine.shape
    arrays, places, held = sources(w)
    outs = pl.pallas_call(
        functools.partial(qkv_kernel, places=places),
        out_shape=[
            jax.ShapeDtypeStruct((rows, head_dim), jnp.bfloat16),
            jax.ShapeDtypeStruct((rows, 2 * head_dim), jnp.bfloat16),
        ]
        + held,
        in_specs=[SMEM] + [VMEM] * (6 + len(arrays)),
        out_specs=[VMEM] * (2 + len(held)),
        compiler_params=PARAMS,
        cost_estimate=project_cost(rows),
    )(place, own, other, q_gain[None, :], k_gain[None, :], cosine, sine, *arrays)
    return outs[0], outs[1], outs[2] if held else w


def mlp_kernel(place_ref, own_ref, other_ref, *refs, places):
    w_refs, held = (refs[:-1], None) if places is None else (refs[:-2], refs[-1])
    hidden = projected(places, place_ref, own_ref, other_ref, w_refs, held)
    refs[len(w_refs)][...] = jax.nn.gelu(hidden, approximate=True).astype(jnp.bfloat16)


def project_mlp(place, own, other, w):
    rows = 2 * own.shape[0]
    arrays, places, held = sources(w)
    outs = pl.pallas_call(
        functools.partial(mlp_kernel, places=places),
        out_shape=[jax.ShapeDtypeStruct((rows, arrays[0].shape[-1]), jnp.bfloat16)] + held,
        in_specs=[SMEM] + [VMEM] * (2 + len(arrays)),
        out_specs=[VMEM] * (1 + len(held)),
        compiler_params=PARAMS,
        cost_estimate=project_cost(rows),
    )(place, own, other, *arrays)
    return outs[0], outs[1] if held else w


def unpack(packed):
    third = packed.shape[-1] // 3
    return jnp.concatenate([packed[:, i * third : (i + 1) * third] for i in range(3)], 0)


def attend_kernel(place_ref, q_ref, fresh_ref, *refs, old_places, first_key):
    old_refs, (out_ref, scores_ref) = refs[:-2], refs[-2:]
    rows, head_dim = q_ref.shape
    half = rows // 2
    zl, y = place_ref[0], place_ref[1]
    q = q_ref[...]
    scale = 1.0 / head_dim**0.5
    dims = (((1,), (1,)), ((), ()))
    row_patch = lax.broadcasted_iota(jnp.int32, (rows, rows), 0) // half
    col_patch = lax.broadcasted_iota(jnp.int32, (rows, rows), 1) // half
    same = row_patch == col_patch

    def old_keys(n):
        if old_places is None:
            chip = lax.rem(zl + n // NY, NZ) * NY + lax.rem(y + n % NY, NY)
            return unpack(old_refs[0][chip, first_key:, :])
        i, at, _, _ = old_places[n]
        return old_refs[i][at : at + rows, :head_dim]

    def old_values(n):
        if old_places is None:
            at = n % NY * rows
            return old_refs[1 + n // NY][at : at + rows, :]
        i, at, _, _ = old_places[n]
        return old_refs[i][at : at + rows, head_dim:]

    first = jnp.where(
        same,
        lax.dot_general(q, fresh_ref[:, :head_dim], dims, preferred_element_type=jnp.float32)
        * scale,
        -1e30,
    )
    scores_ref[0] = first
    top = jnp.max(first, axis=1, keepdims=True)
    chips = NZ * NY
    for n in range(chips):
        s = (
            lax.dot_general(q, old_keys(n), dims, preferred_element_type=jnp.float32)
            * scale
        )
        if n == 0:
            s = jnp.where(same, -1e30, s)
        scores_ref[n + 1] = s
        top = jnp.maximum(top, jnp.max(s, axis=1, keepdims=True))
    total = jnp.zeros((rows, 1), jnp.float32)
    mixed = jnp.zeros((rows, head_dim), jnp.float32)
    for n in range(chips + 1):
        e = jnp.exp(scores_ref[n] - top)
        total = total + jnp.sum(e, axis=1, keepdims=True)
        mixed = mixed + jnp.dot(
            e.astype(jnp.bfloat16),
            old_values(n - 1) if n else fresh_ref[:, head_dim:],
            preferred_element_type=jnp.float32,
        )
    out_ref[...] = (mixed / total).astype(jnp.bfloat16)


def attend(place, queries, fresh, old, first_key=0):
    rows, head_dim = queries.shape
    chips = NZ * NY
    arrays, places = (old.arrays, old.places) if isinstance(old, Spread) else (old, None)
    return pl.pallas_call(
        functools.partial(attend_kernel, old_places=places, first_key=first_key),
        out_shape=jax.ShapeDtypeStruct((rows, head_dim), jnp.bfloat16),
        in_specs=[SMEM] + [VMEM] * (2 + len(arrays)),
        out_specs=VMEM,
        scratch_shapes=[pltpu.VMEM((chips + 1, rows, rows), jnp.float32)],
        compiler_params=PARAMS,
        cost_estimate=pl.CostEstimate(
            flops=4 * rows * rows * chips * head_dim,
            bytes_accessed=4 * rows * chips * head_dim,
            transcendentals=rows * rows * chips,
        ),
    )(place, queries, fresh, *arrays)


def output_kernel(place_ref, attended_ref, act_ref, *refs, places, arrays):
    back_refs, refs = refs[:arrays], refs[arrays:]
    own_refs, other_refs, refs = refs[:NX], refs[NX : 2 * NX], refs[2 * NX :]
    half = attended_ref.shape[0] // 2
    back_ref = refs[0] if places else back_refs[0]
    if places:
        arrange(places, back_refs, back_ref, place_ref[0], place_ref[1])
    back_rows = back_ref.shape[1] * 3 // 4
    attended, activated = attended_ref[...], act_ref[...]
    dims = (((1,), (1,)), ((), ()))
    for k in range(NX):
        at = lax.rem(place_ref[2] + k, NX) * NY
        w_mlp = back_ref[pl.ds(at, NY), :back_rows, :].reshape(NY * back_rows, -1)
        w_att = jnp.concatenate([unpack(back_ref[at + j, back_rows:, :]) for j in range(NY)], 0)
        part = lax.dot_general(activated, w_mlp, dims, preferred_element_type=jnp.float32)
        part = part + lax.dot_general(
            attended, w_att, dims, preferred_element_type=jnp.float32
        )
        own_refs[k][...] = part[:half]
        other_refs[k][...] = part[half:].astype(jnp.bfloat16)


def output(place, attended, activated, back, width):
    rows = attended.shape[0]
    block = width // NX
    arrays, places, held = sources(back)
    kinds = [jnp.float32] * NX + [jnp.bfloat16] * NX
    outs = pl.pallas_call(
        functools.partial(output_kernel, places=places, arrays=len(arrays)),
        out_shape=[jax.ShapeDtypeStruct((rows // 2, block), kind) for kind in kinds] + held,
        in_specs=[SMEM] + [VMEM] * (2 + len(arrays)),
        out_specs=[VMEM] * (len(kinds) + len(held)),
        compiler_params=PARAMS,
        cost_estimate=pl.CostEstimate(
            flops=2 * rows * width * 512, bytes_accessed=2 * width * 512, transcendentals=0
        ),
    )(place, attended, activated, *arrays)
    return outs[:NX], outs[NX : 2 * NX], outs[2 * NX] if held else back


def layer_norm(current, mod_ref, entry):
    centred = current - jnp.mean(current, axis=-1, keepdims=True)
    variance = jnp.mean(centred * centred, axis=-1, keepdims=True)
    mod = mod_ref[entry]
    return (
        centred * lax.rsqrt(variance + epsilon) * (1.0 + mod[1:2, :]) + mod[0:1, :]
    ).astype(jnp.bfloat16)


def norm_kernel(times_ref, cur_ref, mod_ref, out_ref):
    out_ref[...] = layer_norm(cur_ref[...], mod_ref, times_ref[0])


def norm(timesteps, current, mod_table):
    rows, width = current.shape
    whole = pl.BlockSpec((rows // 3, width), lambda i: (i, 0))
    return pl.pallas_call(
        norm_kernel,
        out_shape=jax.ShapeDtypeStruct(current.shape, jnp.bfloat16),
        grid=(3,),
        in_specs=[SMEM, whole, pl.BlockSpec(mod_table.shape, lambda i: (0, 0, 0))],
        out_specs=whole,
        compiler_params=PARAMS,
        cost_estimate=pl.CostEstimate(
            flops=10 * current.size, bytes_accessed=6 * current.size, transcendentals=0
        ),
    )(timesteps, current, mod_table)


def update_kernel(place_ref, times_ref, sigma_ref, cur_ref, mod_ref, *refs, step):
    pieces, (out_a, out_b, branch_ref) = refs[:NX], refs[NX:]
    block = pieces[0].shape[1]
    for k in range(NX):
        at = pl.multiple_of(lax.rem(place_ref[2] + k, NX) * block, block)
        branch_ref[:, pl.ds(at, block)] = pieces[k][...].astype(jnp.float32)
    now, later = times_ref[step], times_ref[step + 1]
    current = cur_ref[...]
    velocity = current + mod_ref[now][2:3, :] * branch_ref[...]
    current = current + (sigma_ref[later] - sigma_ref[now]) * velocity
    if step + 1 == STEPS:
        out_a[...] = velocity
        out_b[...] = current
    else:
        out_a[...] = current
        out_b[...] = layer_norm(current, mod_ref, later)


def update(place, timesteps, sigmas, current, mod_table, pieces, step):
    rows, width = current.shape
    tile = rows // 3
    block = width // NX
    last = step + 1 == STEPS
    whole = pl.BlockSpec((tile, width), lambda i: (i, 0))
    return pl.pallas_call(
        functools.partial(update_kernel, step=step),
        out_shape=[
            jax.ShapeDtypeStruct(current.shape, jnp.float32),
            jax.ShapeDtypeStruct(current.shape, jnp.float32 if last else jnp.bfloat16),
        ],
        grid=(rows // tile,),
        in_specs=[SMEM] * 3
        + [whole, pl.BlockSpec(mod_table.shape, lambda i: (0, 0, 0))]
        + [pl.BlockSpec((tile, block), lambda i: (i, 0))] * NX,
        out_specs=[whole] * 2,
        scratch_shapes=[pltpu.VMEM((tile, width), jnp.float32)],
        compiler_params=PARAMS,
        cost_estimate=pl.CostEstimate(
            flops=20 * current.size, bytes_accessed=14 * current.size, transcendentals=0
        ),
    )(place, timesteps, sigmas, current, mod_table, *pieces)


def local(
    latent, timesteps, sigmas, mod_table, w_in, w_out, q_gain, k_gain, stale_keys, stale_values
):
    own_rows, width = latent.shape
    head_dim = q_gain.shape[0]
    patch = lax.axis_index("patch")
    c = patch % NC
    y = (patch // NC) % NY
    zl = patch // (NC * NY)
    x = lax.axis_index("tensor") % NX
    first = c == 0
    block = width // NY
    text_count = own_rows * lax.axis_size("patch") // 9

    def keep_and_send(for_core_0, for_core_1):
        return jnp.where(first, for_core_0, for_core_1), jnp.where(first, for_core_1, for_core_0)

    def in_core_order(keep, other):
        return jnp.where(
            first, jnp.concatenate([keep, other], 0), jnp.concatenate([other, keep], 0)
        )

    inner = 2 * head_dim
    hidden = (w_in.shape[1] - 3 * inner) // 2

    def qkv_columns(j):
        return jnp.concatenate(
            [w_in[:, i * inner + j * head_dim : i * inner + (j + 1) * head_dim] for i in range(3)], 1
        )

    def mlp_columns(j):
        return w_in[:, 3 * inner + j * hidden : 3 * inner + (j + 1) * hidden]

    def out_columns(j):
        return jnp.concatenate(
            [
                out_t[:, j * head_dim : (j + 1) * head_dim],
                out_t[:, inner + j * hidden : inner + (j + 1) * hidden],
            ],
            1,
        )

    def old_columns(j):
        return jnp.concatenate(
            [a[:, j * head_dim : (j + 1) * head_dim] for a in (stale_keys, stale_values)], 1
        )

    place = jnp.stack([zl, y, x])
    cat = functools.partial(jnp.concatenate, axis=0)

    keep, send = keep_and_send(qkv_columns(0), qkv_columns(1))
    other = swap_core(send)
    qkv_line = line_pieces(in_core_order(keep, other))
    stale_keys, stale_values = after((stale_keys, stale_values), qkv_line[1])
    keep, send = keep_and_send(old_columns(0), old_columns(1))
    old = cat([keep, swap_core(send)])
    old_values = old[:, head_dim:]
    old_values = [old_values] + [from_y(old_values, k) for k in range(1, NY)]
    w_in = after(w_in, old)
    keep, send = keep_and_send(mlp_columns(0), mlp_columns(1))
    mlp_block = cat([in_core_order(keep, swap_core(send)), pack(old[:, :head_dim])])

    qkv_message = cat(qkv_line)
    half = qkv_message.shape[0] // 2
    ahead_1, behind_1 = from_y(qkv_message, 1), from_y(qkv_message, NY - 1)
    mlp_line = line_pieces(after(mlp_block, (qkv_line, old_values)))
    w_out, patch, latent = after((w_out, patch, latent), mlp_line[1])
    first_normed = norm(timesteps, latent, mod_table)
    normed = first_normed, swap_core(first_normed)
    out_t = w_out.T
    back_rows = 2 * out_t.shape[0]
    cosine_table, sine_table = rope_tables(
        patch, patch + 1 - 2 * c, 2 * own_rows, head_dim, text_count
    )
    keep, send = keep_and_send(out_columns(0), out_columns(1))
    out_block = in_core_order(keep, swap_core(send))
    back_block = cat([out_block[:, head_dim:], pack(out_block[:, :head_dim])])

    mlp_message = cat(mlp_line)
    mlp_message, ahead_1, behind_1, back_block = after(
        (mlp_message, ahead_1, behind_1, back_block), normed
    )
    ahead_2, behind_2 = from_y(mlp_message, 1), from_y(mlp_message, NY - 1)
    back_line = line_pieces(after(back_block, (ahead_1, behind_1, mlp_message)))
    ahead_1h = from_y(after(ahead_1[half:], back_line[1]), 1)
    behind_1h = from_y(after(behind_1[:half], ahead_2), NY - 1)

    back_message = cat(back_line)
    values_message = cat(old_values)
    back_message, values_message, ahead_2, behind_2 = after(
        (back_message, values_message, ahead_2, behind_2), (ahead_1h, behind_1h)
    )
    ahead_3, behind_3 = from_y(back_message, 1), from_y(back_message, NY - 1)
    old_values = line_pieces(after(values_message, (ahead_2, behind_2, back_message)))
    half = mlp_message.shape[0] // 2
    ahead_2h = from_y(after(ahead_2[half:], old_values[1]), 1)
    behind_2h = from_y(after(behind_2[:half], old_values[3]), NY - 1)
    w_qkv = Spread(qkv_line, (ahead_1, 0), (behind_1, 0), (ahead_1h, 0), (behind_1h, 0))
    w_mlp = Spread(mlp_line, (ahead_2, 0), (behind_2, 0), (ahead_2h, 0), (behind_2h, 0))

    def wave_4(fresh):
        ahead, behind = after((ahead_3, behind_3), (fresh, old_values, ahead_2h, behind_2h))
        half = back_message.shape[0] // 2
        ahead_3h = from_y(ahead[half:], 1)
        behind_3h = from_y(behind[:half], NY - 1)
        return Spread(back_line, (ahead, 0), (behind, 0), (ahead_3h, 0), (behind_3h, 0))

    current = latent

    for denoise in range(STEPS):
        last = denoise + 1 == STEPS
        queries, fresh, w_qkv = project_qkv(
            place, *normed, w_qkv, q_gain, k_gain, cosine_table, sine_table
        )
        if not last:
            w_back = wave_4(fresh)
        activated, w_mlp = project_mlp(place, *normed, w_mlp)
        old = old if last else [w_mlp] + old_values
        attended = attend(place, queries, fresh, old, back_rows)
        if not last:
            new_line = line_pieces(after(fresh, attended))
            new_message = cat(new_line)
            new_ahead, new_behind = from_y(new_message, 1), from_y(new_message, NY - 1)
        own, other, w_back = output(place, attended, activated, w_back, width)
        blocks = [
            (own[k] + swap_core(other[k]).astype(jnp.float32)).astype(jnp.bfloat16)
            for k in range(NX)
        ]
        total = blocks[0].astype(jnp.float32)
        for k in [2, 1, 3]:
            total = total + from_x(blocks[k], NX - k).astype(jnp.float32)
        half_sum = total.astype(jnp.bfloat16)
        total = half_sum.astype(jnp.float32) + swap_zh(half_sum).astype(jnp.float32)
        done = total.astype(jnp.bfloat16)
        if not last:
            done, new_ahead, new_behind = after((done, new_ahead, new_behind), done)
            half = new_message.shape[0] // 2
            new_halves = from_y(new_ahead[half:], 1), from_y(new_behind[:half], NY - 1)
            old = Spread(
                new_line,
                (new_ahead, 0),
                (new_behind, 0),
                (new_halves[0], 0),
                (new_halves[1], 0),
            )
        pieces = [done] + [from_x(done, k) for k in range(1, NX)]
        if not last:
            pieces = after(pieces, new_halves)
        new = update(place, timesteps, sigmas, current, mod_table, pieces, denoise)
        if last:
            return new
        current, normed = new
        normed = normed, swap_core(normed)


def solution(mesh):
    return jax.shard_map(
        local,
        mesh=mesh,
        in_specs=(
            P("patch", None),
            P(),
            P(),
            P(),
            P("patch", "tensor"),
            P("tensor", "patch"),
            P(),
            P(),
            P("patch", "tensor"),
            P("patch", "tensor"),
        ),
        out_specs=(P("patch", None), P("patch", None)),
        check_vma=False,
    )
```

```python
import functools

import jax
import numpy as np
import jax.numpy as jnp
from jax import lax
from jax.experimental import pallas as pl
from jax.experimental.pallas import tpu as pltpu
from jax.sharding import PartitionSpec as P

STEPS = 2
GRID = 64
epsilon = 1e-06

VMEM = pl.BlockSpec(memory_space=pltpu.VMEM)
SMEM = pl.BlockSpec(memory_space=pltpu.SMEM)
ANY = pl.BlockSpec(memory_space=pl.ANY)
PARAMS = pltpu.CompilerParams(vmem_limit_bytes=40 * 1024 * 1024)

NZ, NY, NC, NH, NX = 4, 4, 2, 2, 4
AXES = ("patch", "tensor")


def flat(zl, y, c, zh, x):
    return (((zl * NY + y) * NC + c) * NH + zh) * NX + x


def pairs(move):
    out = []
    for zl in range(NZ):
        for y in range(NY):
            for c in range(NC):
                for zh in range(NH):
                    for x in range(NX):
                        out.append((flat(zl, y, c, zh, x), flat(*move(zl, y, c, zh, x))))
    return out


def from_z(a, k):
    return lax.ppermute(a, AXES, pairs(lambda zl, y, c, zh, x: ((zl - k) % NZ, y, c, zh, x)))


def from_y(a, k):
    return lax.ppermute(a, AXES, pairs(lambda zl, y, c, zh, x: (zl, (y - k) % NY, c, zh, x)))


def swap_y(a):
    return lax.ppermute(a, AXES, pairs(lambda zl, y, c, zh, x: (zl, y ^ 1, c, zh, x)))


def flip_y(a):
    return lax.ppermute(a, AXES, pairs(lambda zl, y, c, zh, x: (zl, NY - 1 - y, c, zh, x)))


def from_x(a, k):
    return lax.ppermute(a, AXES, pairs(lambda zl, y, c, zh, x: (zl, y, c, zh, (x - k) % NX)))


def swap_core(a):
    return lax.ppermute(a, AXES, pairs(lambda zl, y, c, zh, x: (zl, y, 1 - c, zh, x)))


def swap_zh(a):
    return lax.ppermute(a, AXES, pairs(lambda zl, y, c, zh, x: (zl, y, c, 1 - zh, x)))


def frequencies(width_axis):
    return 1.0 / np.power(10000.0, np.arange(0, width_axis, 2) / width_axis)


def rope_rates(head_dim):
    first_width = head_dim // 8
    other_width = (head_dim - first_width) // 2
    none, rates = np.zeros(first_width // 2), frequencies(other_width)
    by_row = np.concatenate([none, rates, 0 * rates])
    by_column = np.concatenate([none, 0 * rates, rates])
    return np.repeat(np.stack([by_row, by_column]), 2, axis=1).astype(np.float32)


def rope_kernel(place_ref, rates_ref, cos_ref, sin_ref, *, text_count):
    rows, head_dim = cos_ref.shape
    half = rows // 2
    patch, other = place_ref[0], place_ref[1]
    index = lax.broadcasted_iota(jnp.int32, (rows, head_dim), 0)
    token = jnp.where(index < half, patch * half + index, other * half + index - half)
    image = jnp.maximum(token - text_count, 0)
    row = (image // GRID).astype(jnp.float32)
    column = (image % GRID).astype(jnp.float32)
    angles = row * rates_ref[0:1, :] + column * rates_ref[1:2, :]
    parity = lax.broadcasted_iota(jnp.int32, (rows, head_dim), 1) % 2
    cos_ref[...] = jnp.cos(angles)
    sin_ref[...] = jnp.sin(angles) * jnp.where(parity == 0, -1.0, 1.0)


def rope_tables(patch, other, rows, head_dim, text_count):
    return pl.pallas_call(
        functools.partial(rope_kernel, text_count=text_count),
        out_shape=[jax.ShapeDtypeStruct((rows, head_dim), jnp.float32)] * 2,
        in_specs=[SMEM, VMEM],
        out_specs=[VMEM] * 2,
        compiler_params=PARAMS,
    )(jnp.stack([patch, other]), jnp.asarray(rope_rates(head_dim)))


def after(array, done):
    return lax.optimization_barrier((array, done))[0]


def line_pieces(block):
    return [block] + [from_z(block, k) for k in range(1, NZ)]


def line_of(block):
    return jnp.concatenate(line_pieces(block), 0)


def pack(array):
    rows = array.shape[0] // 3
    return jnp.concatenate([array[i * rows : (i + 1) * rows] for i in range(3)], 1)


class Spread:
    def __init__(self, line, ahead, behind, ahead_half, behind_half):
        self.rows, self.columns = line[0].shape
        self.arrays = line + [s[0] for s in (ahead, behind, ahead_half, behind_half)]
        ahead, behind, ahead_half, behind_half = (
            s[1] for s in (ahead, behind, ahead_half, behind_half)
        )
        self.places = [(kz, 0, kz, 0) for kz in range(NZ)]
        self.places += [(NZ, ahead + kz * self.rows, kz, 1) for kz in range(NZ)]
        self.places += [(NZ + 1, behind + kz * self.rows, kz, NY - 1) for kz in range(NZ)]
        for kz in range(NZ):
            late = kz >= NZ // 2
            at = (ahead_half if late else behind_half) + kz % (NZ // 2) * self.rows
            self.places.append((NZ + 2 if late else NZ + 3, at, kz, 2))


def arrange(places, refs, held, zl, y):
    rows = held.shape[1]
    for n, at, kz, ky in places:
        chip = lax.rem(zl + kz, NZ) * NY + lax.rem(y + ky, NY)
        held[chip] = refs[n][at : at + rows, :]


def turn(columns, gain, cosine, sine):
    scaled = (
        columns
        * lax.rsqrt(jnp.mean(columns * columns, axis=-1, keepdims=True) + epsilon)
        * gain
    )
    width = columns.shape[1]
    parity = lax.broadcasted_iota(jnp.int32, columns.shape, 1) % 2
    swapped = jnp.where(
        parity == 0, pltpu.roll(scaled, width - 1, 1), pltpu.roll(scaled, 1, 1)
    )
    return (scaled * cosine + swapped * sine).astype(jnp.bfloat16)


def arranged(spread):
    return jax.ShapeDtypeStruct((NZ * NY, spread.rows, spread.columns), jnp.bfloat16)


def projected(places, place_ref, own_ref, other_ref, w_refs, held):
    if places is None:
        held = w_refs[0]
    else:
        arrange(places, w_refs, held, place_ref[0], place_ref[1])
    normed = jnp.concatenate([own_ref[...], other_ref[...]], 0)
    rows = normed.shape[1] // held.shape[0]
    w = held[:, :rows, :].reshape(normed.shape[1], held.shape[2])
    return jnp.dot(normed, w, preferred_element_type=jnp.float32)


def qkv_kernel(
    place_ref, own_ref, other_ref, qg_ref, kg_ref, cos_ref, sin_ref, *refs, places
):
    w_refs, held = (refs[:-2], None) if places is None else (refs[:-3], refs[-1])
    q_ref, fresh_ref = refs[len(w_refs) : len(w_refs) + 2]
    head_dim = q_ref.shape[1]
    qkv = projected(places, place_ref, own_ref, other_ref, w_refs, held)
    cosine, sine = cos_ref[...], sin_ref[...]
    q_ref[...] = turn(qkv[:, :head_dim], qg_ref[...], cosine, sine)
    fresh_ref[:, :head_dim] = turn(qkv[:, head_dim : 2 * head_dim], kg_ref[...], cosine, sine)
    fresh_ref[:, head_dim:] = qkv[:, 2 * head_dim :].astype(jnp.bfloat16)


def sources(w):
    if isinstance(w, Spread):
        return w.arrays, w.places, [arranged(w)]
    return [w], None, []


def project_cost(rows):
    size = 3072 * 384
    return pl.CostEstimate(flops=2 * rows * size, bytes_accessed=2 * size, transcendentals=0)


def project_qkv(place, own, other, w, q_gain, k_gain, cosine, sine):
    rows, head_dim = cosine.shape
    arrays, places, held = sources(w)
    outs = pl.pallas_call(
        functools.partial(qkv_kernel, places=places),
        out_shape=[
            jax.ShapeDtypeStruct((rows, head_dim), jnp.bfloat16),
            jax.ShapeDtypeStruct((rows, 2 * head_dim), jnp.bfloat16),
        ]
        + held,
        in_specs=[SMEM] + [VMEM] * (6 + len(arrays)),
        out_specs=[VMEM] * (2 + len(held)),
        compiler_params=PARAMS,
        cost_estimate=project_cost(rows),
    )(place, own, other, q_gain[None, :], k_gain[None, :], cosine, sine, *arrays)
    return outs[0], outs[1], outs[2] if held else w


def mlp_kernel(place_ref, own_ref, other_ref, *refs, places):
    w_refs, held = (refs[:-1], None) if places is None else (refs[:-2], refs[-1])
    hidden = projected(places, place_ref, own_ref, other_ref, w_refs, held)
    refs[len(w_refs)][...] = jax.nn.gelu(hidden, approximate=True).astype(jnp.bfloat16)


def project_mlp(place, own, other, w):
    rows = 2 * own.shape[0]
    arrays, places, held = sources(w)
    outs = pl.pallas_call(
        functools.partial(mlp_kernel, places=places),
        out_shape=[jax.ShapeDtypeStruct((rows, arrays[0].shape[-1]), jnp.bfloat16)] + held,
        in_specs=[SMEM] + [VMEM] * (2 + len(arrays)),
        out_specs=[VMEM] * (1 + len(held)),
        compiler_params=PARAMS,
        cost_estimate=project_cost(rows),
    )(place, own, other, *arrays)
    return outs[0], outs[1] if held else w


def unpack(packed):
    third = packed.shape[-1] // 3
    return jnp.concatenate([packed[:, i * third : (i + 1) * third] for i in range(3)], 0)


def attend_kernel(place_ref, q_ref, fresh_ref, *refs, old_places, first_key):
    old_refs, (out_ref, scores_ref) = refs[:-2], refs[-2:]
    rows, head_dim = q_ref.shape
    half = rows // 2
    zl, y = place_ref[0], place_ref[1]
    q = q_ref[...]
    scale = 1.0 / head_dim**0.5
    dims = (((1,), (1,)), ((), ()))
    row_patch = lax.broadcasted_iota(jnp.int32, (rows, rows), 0) // half
    col_patch = lax.broadcasted_iota(jnp.int32, (rows, rows), 1) // half
    same = row_patch == col_patch

    def old_keys(n):
        if old_places is None:
            chip = lax.rem(zl + n // NY, NZ) * NY + lax.rem(y + n % NY, NY)
            return unpack(old_refs[0][chip, first_key:, :])
        i, at, _, _ = old_places[n]
        return old_refs[i][at : at + rows, :head_dim]

    def old_values(n):
        if old_places is None:
            at = n % NY * rows
            return old_refs[1 + n // NY][at : at + rows, :]
        i, at, _, _ = old_places[n]
        return old_refs[i][at : at + rows, head_dim:]

    first = jnp.where(
        same,
        lax.dot_general(q, fresh_ref[:, :head_dim], dims, preferred_element_type=jnp.float32)
        * scale,
        -1e30,
    )
    scores_ref[0] = first
    top = jnp.max(first, axis=1, keepdims=True)
    chips = NZ * NY
    for n in range(chips):
        s = (
            lax.dot_general(q, old_keys(n), dims, preferred_element_type=jnp.float32)
            * scale
        )
        if n == 0:
            s = jnp.where(same, -1e30, s)
        scores_ref[n + 1] = s
        top = jnp.maximum(top, jnp.max(s, axis=1, keepdims=True))
    total = jnp.zeros((rows, 1), jnp.float32)
    mixed = jnp.zeros((rows, head_dim), jnp.float32)
    for n in range(chips + 1):
        e = jnp.exp(scores_ref[n] - top)
        total = total + jnp.sum(e, axis=1, keepdims=True)
        mixed = mixed + jnp.dot(
            e.astype(jnp.bfloat16),
            old_values(n - 1) if n else fresh_ref[:, head_dim:],
            preferred_element_type=jnp.float32,
        )
    out_ref[...] = (mixed / total).astype(jnp.bfloat16)


def attend(place, queries, fresh, old, first_key=0):
    rows, head_dim = queries.shape
    chips = NZ * NY
    arrays, places = (old.arrays, old.places) if isinstance(old, Spread) else (old, None)
    return pl.pallas_call(
        functools.partial(attend_kernel, old_places=places, first_key=first_key),
        out_shape=jax.ShapeDtypeStruct((rows, head_dim), jnp.bfloat16),
        in_specs=[SMEM] + [VMEM] * (2 + len(arrays)),
        out_specs=VMEM,
        scratch_shapes=[pltpu.VMEM((chips + 1, rows, rows), jnp.float32)],
        compiler_params=PARAMS,
        cost_estimate=pl.CostEstimate(
            flops=4 * rows * rows * chips * head_dim,
            bytes_accessed=4 * rows * chips * head_dim,
            transcendentals=rows * rows * chips,
        ),
    )(place, queries, fresh, *arrays)


def output_kernel(place_ref, attended_ref, act_ref, *refs, places, arrays):
    back_refs, refs = refs[:arrays], refs[arrays:]
    own_refs, other_refs, refs = refs[:NX], refs[NX : 2 * NX], refs[2 * NX :]
    half = attended_ref.shape[0] // 2
    back_ref = refs[0] if places else back_refs[0]
    if places:
        arrange(places, back_refs, back_ref, place_ref[0], place_ref[1])
    back_rows = back_ref.shape[1] * 3 // 4
    attended, activated = attended_ref[...], act_ref[...]
    dims = (((1,), (1,)), ((), ()))
    for k in range(NX):
        at = lax.rem(place_ref[2] + k, NX) * NY
        w_mlp = back_ref[pl.ds(at, NY), :back_rows, :].reshape(NY * back_rows, -1)
        w_att = jnp.concatenate([unpack(back_ref[at + j, back_rows:, :]) for j in range(NY)], 0)
        part = lax.dot_general(activated, w_mlp, dims, preferred_element_type=jnp.float32)
        part = part + lax.dot_general(
            attended, w_att, dims, preferred_element_type=jnp.float32
        )
        own_refs[k][...] = part[:half]
        other_refs[k][...] = part[half:].astype(jnp.bfloat16)


def output(place, attended, activated, back, width):
    rows = attended.shape[0]
    block = width // NX
    arrays, places, held = sources(back)
    kinds = [jnp.float32] * NX + [jnp.bfloat16] * NX
    outs = pl.pallas_call(
        functools.partial(output_kernel, places=places, arrays=len(arrays)),
        out_shape=[jax.ShapeDtypeStruct((rows // 2, block), kind) for kind in kinds] + held,
        in_specs=[SMEM] + [VMEM] * (2 + len(arrays)),
        out_specs=[VMEM] * (len(kinds) + len(held)),
        compiler_params=PARAMS,
        cost_estimate=pl.CostEstimate(
            flops=2 * rows * width * 512, bytes_accessed=2 * width * 512, transcendentals=0
        ),
    )(place, attended, activated, *arrays)
    return outs[:NX], outs[NX : 2 * NX], outs[2 * NX] if held else back


def layer_norm(current, mod_ref, entry):
    centred = current - jnp.mean(current, axis=-1, keepdims=True)
    variance = jnp.mean(centred * centred, axis=-1, keepdims=True)
    mod = mod_ref[entry]
    return (
        centred * lax.rsqrt(variance + epsilon) * (1.0 + mod[1:2, :]) + mod[0:1, :]
    ).astype(jnp.bfloat16)


def norm_kernel(times_ref, cur_ref, mod_ref, out_ref):
    out_ref[...] = layer_norm(cur_ref[...], mod_ref, times_ref[0])


def norm(timesteps, current, mod_table):
    rows, width = current.shape
    whole = pl.BlockSpec((rows // 3, width), lambda i: (i, 0))
    return pl.pallas_call(
        norm_kernel,
        out_shape=jax.ShapeDtypeStruct(current.shape, jnp.bfloat16),
        grid=(3,),
        in_specs=[SMEM, whole, pl.BlockSpec(mod_table.shape, lambda i: (0, 0, 0))],
        out_specs=whole,
        compiler_params=PARAMS,
        cost_estimate=pl.CostEstimate(
            flops=10 * current.size, bytes_accessed=6 * current.size, transcendentals=0
        ),
    )(timesteps, current, mod_table)


def update_kernel(place_ref, times_ref, sigma_ref, cur_ref, mod_ref, *refs, step):
    pieces, (out_a, out_b, branch_ref) = refs[:NX], refs[NX:]
    block = pieces[0].shape[1]
    for k in range(NX):
        at = pl.multiple_of(lax.rem(place_ref[2] + k, NX) * block, block)
        branch_ref[:, pl.ds(at, block)] = pieces[k][...].astype(jnp.float32)
    now, later = times_ref[step], times_ref[step + 1]
    current = cur_ref[...]
    velocity = current + mod_ref[now][2:3, :] * branch_ref[...]
    current = current + (sigma_ref[later] - sigma_ref[now]) * velocity
    if step + 1 == STEPS:
        out_a[...] = velocity
        out_b[...] = current
    else:
        out_a[...] = current
        out_b[...] = layer_norm(current, mod_ref, later)


def update(place, timesteps, sigmas, current, mod_table, pieces, step):
    rows, width = current.shape
    tile = rows // 3
    block = width // NX
    last = step + 1 == STEPS
    whole = pl.BlockSpec((tile, width), lambda i: (i, 0))
    return pl.pallas_call(
        functools.partial(update_kernel, step=step),
        out_shape=[
            jax.ShapeDtypeStruct(current.shape, jnp.float32),
            jax.ShapeDtypeStruct(current.shape, jnp.float32 if last else jnp.bfloat16),
        ],
        grid=(rows // tile,),
        in_specs=[SMEM] * 3
        + [whole, pl.BlockSpec(mod_table.shape, lambda i: (0, 0, 0))]
        + [pl.BlockSpec((tile, block), lambda i: (i, 0))] * NX,
        out_specs=[whole] * 2,
        scratch_shapes=[pltpu.VMEM((tile, width), jnp.float32)],
        compiler_params=PARAMS,
        cost_estimate=pl.CostEstimate(
            flops=20 * current.size, bytes_accessed=14 * current.size, transcendentals=0
        ),
    )(place, timesteps, sigmas, current, mod_table, *pieces)


def local(
    latent, timesteps, sigmas, mod_table, w_in, w_out, q_gain, k_gain, stale_keys, stale_values
):
    own_rows, width = latent.shape
    head_dim = q_gain.shape[0]
    patch = lax.axis_index("patch")
    c = patch % NC
    y = (patch // NC) % NY
    zl = patch // (NC * NY)
    x = lax.axis_index("tensor") % NX
    first = c == 0
    block = width // NY
    text_count = own_rows * lax.axis_size("patch") // 9

    def keep_and_send(for_core_0, for_core_1):
        return jnp.where(first, for_core_0, for_core_1), jnp.where(first, for_core_1, for_core_0)

    def in_core_order(keep, other):
        return jnp.where(
            first, jnp.concatenate([keep, other], 0), jnp.concatenate([other, keep], 0)
        )

    inner = 2 * head_dim
    hidden = (w_in.shape[1] - 3 * inner) // 2

    def qkv_columns(j):
        return jnp.concatenate(
            [w_in[:, i * inner + j * head_dim : i * inner + (j + 1) * head_dim] for i in range(3)], 1
        )

    def mlp_columns(j):
        return w_in[:, 3 * inner + j * hidden : 3 * inner + (j + 1) * hidden]

    def out_columns(j):
        return jnp.concatenate(
            [
                out_t[:, j * head_dim : (j + 1) * head_dim],
                out_t[:, inner + j * hidden : inner + (j + 1) * hidden],
            ],
            1,
        )

    def old_columns(j):
        return jnp.concatenate(
            [a[:, j * head_dim : (j + 1) * head_dim] for a in (stale_keys, stale_values)], 1
        )

    place = jnp.stack([zl, y, x])
    cat = functools.partial(jnp.concatenate, axis=0)

    keep, send = keep_and_send(qkv_columns(0), qkv_columns(1))
    other = swap_core(send)
    qkv_line = line_pieces(in_core_order(keep, other))
    stale_keys, stale_values = after((stale_keys, stale_values), qkv_line[1])
    keep, send = keep_and_send(old_columns(0), old_columns(1))
    old = cat([keep, swap_core(send)])
    old_values = old[:, head_dim:]
    old_values = [old_values] + [from_y(old_values, k) for k in range(1, NY)]
    w_in = after(w_in, old)
    keep, send = keep_and_send(mlp_columns(0), mlp_columns(1))
    mlp_block = cat([in_core_order(keep, swap_core(send)), pack(old[:, :head_dim])])

    qkv_message = cat(qkv_line)
    half = qkv_message.shape[0] // 2
    ahead_1, behind_1 = from_y(qkv_message, 1), from_y(qkv_message, NY - 1)
    mlp_line = line_pieces(after(mlp_block, (qkv_line, old_values)))
    w_out, patch, latent = after((w_out, patch, latent), mlp_line[1])
    first_normed = norm(timesteps, latent, mod_table)
    normed = first_normed, swap_core(first_normed)
    out_t = w_out.T
    back_rows = 2 * out_t.shape[0]
    cosine_table, sine_table = rope_tables(
        patch, patch + 1 - 2 * c, 2 * own_rows, head_dim, text_count
    )
    keep, send = keep_and_send(out_columns(0), out_columns(1))
    out_block = in_core_order(keep, swap_core(send))
    back_block = cat([out_block[:, head_dim:], pack(out_block[:, :head_dim])])

    mlp_message = cat(mlp_line)
    mlp_message, ahead_1, behind_1, back_block = after(
        (mlp_message, ahead_1, behind_1, back_block), normed
    )
    ahead_2, behind_2 = from_y(mlp_message, 1), from_y(mlp_message, NY - 1)
    near = from_z(back_block, 1)
    ahead_1h = from_y(after(ahead_1[half:], near), 1)
    behind_1h = from_y(after(behind_1[:half], near), NY - 1)
    far = from_z(after(back_block, near), 2)
    back_line = [back_block, near, far, from_z(after(back_block, far), 3)]

    back_message = cat(back_line)
    values_message = cat(old_values)
    back_message, values_message, ahead_2, behind_2 = after(
        (back_message, values_message, ahead_2, behind_2), (ahead_1h, behind_1h)
    )
    ahead_3, behind_3 = from_y(back_message, 1), from_y(back_message, NY - 1)
    half = mlp_message.shape[0] // 2
    near, last_piece = from_z(values_message, 1), from_z(values_message, 3)
    ahead_2h = from_y(ahead_2[half:], 1)
    far = from_z(after(values_message, near), 2)
    behind_2h = from_y(after(behind_2[:half], last_piece), NY - 1)
    old_values = [values_message, near, far, last_piece]
    w_qkv = Spread(qkv_line, (ahead_1, 0), (behind_1, 0), (ahead_1h, 0), (behind_1h, 0))
    w_mlp = Spread(mlp_line, (ahead_2, 0), (behind_2, 0), (ahead_2h, 0), (behind_2h, 0))

    def wave_4(fresh):
        ahead, behind = after((ahead_3, behind_3), (fresh, old_values, ahead_2h, behind_2h))
        half = back_message.shape[0] // 2
        ahead_3h = from_y(ahead[half:], 1)
        behind_3h = from_y(behind[:half], NY - 1)
        return Spread(back_line, (ahead, 0), (behind, 0), (ahead_3h, 0), (behind_3h, 0))

    current = latent

    for denoise in range(STEPS):
        last = denoise + 1 == STEPS
        queries, fresh, w_qkv = project_qkv(
            place, *normed, w_qkv, q_gain, k_gain, cosine_table, sine_table
        )
        if not last:
            w_back = wave_4(fresh)
        activated, w_mlp = project_mlp(place, *normed, w_mlp)
        old = old if last else [w_mlp] + old_values
        attended = attend(place, queries, fresh, old, back_rows)
        if not last:
            new_line = line_pieces(after(fresh, attended))
            new_message = cat(new_line)
            new_ahead, new_behind = from_y(new_message, 1), from_y(new_message, NY - 1)
        own, other, w_back = output(place, attended, activated, w_back, width)
        blocks = [
            (own[k] + swap_core(other[k]).astype(jnp.float32)).astype(jnp.bfloat16)
            for k in range(NX)
        ]
        total = blocks[0].astype(jnp.float32)
        for k in [2, 1, 3]:
            total = total + from_x(blocks[k], NX - k).astype(jnp.float32)
        half_sum = total.astype(jnp.bfloat16)
        total = half_sum.astype(jnp.float32) + swap_zh(half_sum).astype(jnp.float32)
        done = total.astype(jnp.bfloat16)
        if not last:
            done, new_ahead, new_behind = after((done, new_ahead, new_behind), done)
            half = new_message.shape[0] // 2
            new_halves = from_y(new_ahead[half:], 1), from_y(new_behind[:half], NY - 1)
            old = Spread(
                new_line,
                (new_ahead, 0),
                (new_behind, 0),
                (new_halves[0], 0),
                (new_halves[1], 0),
            )
        pieces = [done] + [from_x(done, k) for k in range(1, NX)]
        if not last:
            pieces = after(pieces, new_halves)
        new = update(place, timesteps, sigmas, current, mod_table, pieces, denoise)
        if last:
            return new
        current, normed = new
        normed = normed, swap_core(normed)


def solution(mesh):
    return jax.shard_map(
        local,
        mesh=mesh,
        in_specs=(
            P("patch", None),
            P(),
            P(),
            P(),
            P("patch", "tensor"),
            P("tensor", "patch"),
            P(),
            P(),
            P("patch", "tensor"),
            P("patch", "tensor"),
        ),
        out_specs=(P("patch", None), P("patch", None)),
        check_vma=False,
    )
```

```python
import functools

import jax
import numpy as np
import jax.numpy as jnp
from jax import lax
from jax.experimental import pallas as pl
from jax.experimental.pallas import tpu as pltpu
from jax.sharding import PartitionSpec as P

STEPS = 2
GRID = 64
epsilon = 1e-06

VMEM = pl.BlockSpec(memory_space=pltpu.VMEM)
SMEM = pl.BlockSpec(memory_space=pltpu.SMEM)
ANY = pl.BlockSpec(memory_space=pl.ANY)
PARAMS = pltpu.CompilerParams(vmem_limit_bytes=40 * 1024 * 1024)

NZ, NY, NC, NH, NX = 4, 4, 2, 2, 4
AXES = ("patch", "tensor")


def flat(zl, y, c, zh, x):
    return (((zl * NY + y) * NC + c) * NH + zh) * NX + x


def pairs(move):
    out = []
    for zl in range(NZ):
        for y in range(NY):
            for c in range(NC):
                for zh in range(NH):
                    for x in range(NX):
                        out.append((flat(zl, y, c, zh, x), flat(*move(zl, y, c, zh, x))))
    return out


def from_z(a, k):
    return lax.ppermute(a, AXES, pairs(lambda zl, y, c, zh, x: ((zl - k) % NZ, y, c, zh, x)))


def from_y(a, k):
    return lax.ppermute(a, AXES, pairs(lambda zl, y, c, zh, x: (zl, (y - k) % NY, c, zh, x)))


def swap_y(a):
    return lax.ppermute(a, AXES, pairs(lambda zl, y, c, zh, x: (zl, y ^ 1, c, zh, x)))


def flip_y(a):
    return lax.ppermute(a, AXES, pairs(lambda zl, y, c, zh, x: (zl, NY - 1 - y, c, zh, x)))


def from_x(a, k):
    return lax.ppermute(a, AXES, pairs(lambda zl, y, c, zh, x: (zl, y, c, zh, (x - k) % NX)))


def swap_core(a):
    return lax.ppermute(a, AXES, pairs(lambda zl, y, c, zh, x: (zl, y, 1 - c, zh, x)))


def swap_zh(a):
    return lax.ppermute(a, AXES, pairs(lambda zl, y, c, zh, x: (zl, y, c, 1 - zh, x)))


def frequencies(width_axis):
    return 1.0 / np.power(10000.0, np.arange(0, width_axis, 2) / width_axis)


def rope_rates(head_dim):
    first_width = head_dim // 8
    other_width = (head_dim - first_width) // 2
    none, rates = np.zeros(first_width // 2), frequencies(other_width)
    by_row = np.concatenate([none, rates, 0 * rates])
    by_column = np.concatenate([none, 0 * rates, rates])
    return np.repeat(np.stack([by_row, by_column]), 2, axis=1).astype(np.float32)


def rope_kernel(place_ref, rates_ref, cos_ref, sin_ref, *, text_count):
    rows, head_dim = cos_ref.shape
    half = rows // 2
    patch, other = place_ref[0], place_ref[1]
    index = lax.broadcasted_iota(jnp.int32, (rows, head_dim), 0)
    token = jnp.where(index < half, patch * half + index, other * half + index - half)
    image = jnp.maximum(token - text_count, 0)
    row = (image // GRID).astype(jnp.float32)
    column = (image % GRID).astype(jnp.float32)
    angles = row * rates_ref[0:1, :] + column * rates_ref[1:2, :]
    parity = lax.broadcasted_iota(jnp.int32, (rows, head_dim), 1) % 2
    cos_ref[...] = jnp.cos(angles)
    sin_ref[...] = jnp.sin(angles) * jnp.where(parity == 0, -1.0, 1.0)


def rope_tables(patch, other, rows, head_dim, text_count):
    return pl.pallas_call(
        functools.partial(rope_kernel, text_count=text_count),
        out_shape=[jax.ShapeDtypeStruct((rows, head_dim), jnp.float32)] * 2,
        in_specs=[SMEM, VMEM],
        out_specs=[VMEM] * 2,
        compiler_params=PARAMS,
    )(jnp.stack([patch, other]), jnp.asarray(rope_rates(head_dim)))


def after(array, done):
    return lax.optimization_barrier((array, done))[0]


def line_pieces(block):
    return [block] + [from_z(block, k) for k in range(1, NZ)]


def line_of(block):
    return jnp.concatenate(line_pieces(block), 0)


def pack(array):
    rows = array.shape[0] // 3
    return jnp.concatenate([array[i * rows : (i + 1) * rows] for i in range(3)], 1)


class Spread:
    def __init__(self, line, ahead, behind, ahead_half, behind_half):
        self.rows, self.columns = line[0].shape
        self.arrays = line + [s[0] for s in (ahead, behind, ahead_half, behind_half)]
        ahead, behind, ahead_half, behind_half = (
            s[1] for s in (ahead, behind, ahead_half, behind_half)
        )
        self.places = [(kz, 0, kz, 0) for kz in range(NZ)]
        self.places += [(NZ, ahead + kz * self.rows, kz, 1) for kz in range(NZ)]
        self.places += [(NZ + 1, behind + kz * self.rows, kz, NY - 1) for kz in range(NZ)]
        for kz in range(NZ):
            late = kz >= NZ // 2
            at = (ahead_half if late else behind_half) + kz % (NZ // 2) * self.rows
            self.places.append((NZ + 2 if late else NZ + 3, at, kz, 2))


def arrange(places, refs, held, zl, y):
    rows = held.shape[1]
    for n, at, kz, ky in places:
        chip = lax.rem(zl + kz, NZ) * NY + lax.rem(y + ky, NY)
        held[chip] = refs[n][at : at + rows, :]


def turn(columns, gain, cosine, sine):
    scaled = (
        columns
        * lax.rsqrt(jnp.mean(columns * columns, axis=-1, keepdims=True) + epsilon)
        * gain
    )
    width = columns.shape[1]
    parity = lax.broadcasted_iota(jnp.int32, columns.shape, 1) % 2
    swapped = jnp.where(
        parity == 0, pltpu.roll(scaled, width - 1, 1), pltpu.roll(scaled, 1, 1)
    )
    return (scaled * cosine + swapped * sine).astype(jnp.bfloat16)


def arranged(spread):
    return jax.ShapeDtypeStruct((NZ * NY, spread.rows, spread.columns), jnp.bfloat16)


def projected(places, place_ref, own_ref, other_ref, w_refs, held):
    if places is None:
        held = w_refs[0]
    else:
        arrange(places, w_refs, held, place_ref[0], place_ref[1])
    normed = jnp.concatenate([own_ref[...], other_ref[...]], 0)
    rows = normed.shape[1] // held.shape[0]
    w = held[:, :rows, :].reshape(normed.shape[1], held.shape[2])
    return jnp.dot(normed, w, preferred_element_type=jnp.float32)


def qkv_kernel(
    place_ref, own_ref, other_ref, qg_ref, kg_ref, cos_ref, sin_ref, *refs, places
):
    w_refs, held = (refs[:-2], None) if places is None else (refs[:-3], refs[-1])
    q_ref, fresh_ref = refs[len(w_refs) : len(w_refs) + 2]
    head_dim = q_ref.shape[1]
    qkv = projected(places, place_ref, own_ref, other_ref, w_refs, held)
    cosine, sine = cos_ref[...], sin_ref[...]
    q_ref[...] = turn(qkv[:, :head_dim], qg_ref[...], cosine, sine)
    fresh_ref[:, :head_dim] = turn(qkv[:, head_dim : 2 * head_dim], kg_ref[...], cosine, sine)
    fresh_ref[:, head_dim:] = qkv[:, 2 * head_dim :].astype(jnp.bfloat16)


def sources(w):
    if isinstance(w, Spread):
        return w.arrays, w.places, [arranged(w)]
    return [w], None, []


def project_cost(rows):
    size = 3072 * 384
    return pl.CostEstimate(flops=2 * rows * size, bytes_accessed=2 * size, transcendentals=0)


def project_qkv(place, own, other, w, q_gain, k_gain, cosine, sine):
    rows, head_dim = cosine.shape
    arrays, places, held = sources(w)
    outs = pl.pallas_call(
        functools.partial(qkv_kernel, places=places),
        out_shape=[
            jax.ShapeDtypeStruct((rows, head_dim), jnp.bfloat16),
            jax.ShapeDtypeStruct((rows, 2 * head_dim), jnp.bfloat16),
        ]
        + held,
        in_specs=[SMEM] + [VMEM] * (6 + len(arrays)),
        out_specs=[VMEM] * (2 + len(held)),
        compiler_params=PARAMS,
        cost_estimate=project_cost(rows),
    )(place, own, other, q_gain[None, :], k_gain[None, :], cosine, sine, *arrays)
    return outs[0], outs[1], outs[2] if held else w


def mlp_kernel(place_ref, own_ref, other_ref, *refs, places):
    w_refs, held = (refs[:-1], None) if places is None else (refs[:-2], refs[-1])
    hidden = projected(places, place_ref, own_ref, other_ref, w_refs, held)
    refs[len(w_refs)][...] = jax.nn.gelu(hidden, approximate=True).astype(jnp.bfloat16)


def project_mlp(place, own, other, w):
    rows = 2 * own.shape[0]
    arrays, places, held = sources(w)
    outs = pl.pallas_call(
        functools.partial(mlp_kernel, places=places),
        out_shape=[jax.ShapeDtypeStruct((rows, arrays[0].shape[-1]), jnp.bfloat16)] + held,
        in_specs=[SMEM] + [VMEM] * (2 + len(arrays)),
        out_specs=[VMEM] * (1 + len(held)),
        compiler_params=PARAMS,
        cost_estimate=project_cost(rows),
    )(place, own, other, *arrays)
    return outs[0], outs[1] if held else w


def unpack(packed):
    third = packed.shape[-1] // 3
    return jnp.concatenate([packed[:, i * third : (i + 1) * third] for i in range(3)], 0)


def attend_kernel(place_ref, q_ref, fresh_ref, *refs, old_places, first_key):
    old_refs, (out_ref, scores_ref) = refs[:-2], refs[-2:]
    rows, head_dim = q_ref.shape
    half = rows // 2
    zl, y = place_ref[0], place_ref[1]
    q = q_ref[...]
    scale = 1.0 / head_dim**0.5
    dims = (((1,), (1,)), ((), ()))
    row_patch = lax.broadcasted_iota(jnp.int32, (rows, rows), 0) // half
    col_patch = lax.broadcasted_iota(jnp.int32, (rows, rows), 1) // half
    same = row_patch == col_patch

    def old_keys(n):
        if old_places is None:
            chip = lax.rem(zl + n // NY, NZ) * NY + lax.rem(y + n % NY, NY)
            return unpack(old_refs[0][chip, first_key:, :])
        i, at, _, _ = old_places[n]
        return old_refs[i][at : at + rows, :head_dim]

    def old_values(n):
        if old_places is None:
            at = n % NY * rows
            return old_refs[1 + n // NY][at : at + rows, :]
        i, at, _, _ = old_places[n]
        return old_refs[i][at : at + rows, head_dim:]

    first = jnp.where(
        same,
        lax.dot_general(q, fresh_ref[:, :head_dim], dims, preferred_element_type=jnp.float32)
        * scale,
        -1e30,
    )
    scores_ref[0] = first
    top = jnp.max(first, axis=1, keepdims=True)
    chips = NZ * NY
    for n in range(chips):
        s = (
            lax.dot_general(q, old_keys(n), dims, preferred_element_type=jnp.float32)
            * scale
        )
        if n == 0:
            s = jnp.where(same, -1e30, s)
        scores_ref[n + 1] = s
        top = jnp.maximum(top, jnp.max(s, axis=1, keepdims=True))
    total = jnp.zeros((rows, 1), jnp.float32)
    mixed = jnp.zeros((rows, head_dim), jnp.float32)
    for n in range(chips + 1):
        e = jnp.exp(scores_ref[n] - top)
        total = total + jnp.sum(e, axis=1, keepdims=True)
        mixed = mixed + jnp.dot(
            e.astype(jnp.bfloat16),
            old_values(n - 1) if n else fresh_ref[:, head_dim:],
            preferred_element_type=jnp.float32,
        )
    out_ref[...] = (mixed / total).astype(jnp.bfloat16)


def attend(place, queries, fresh, old, first_key=0):
    rows, head_dim = queries.shape
    chips = NZ * NY
    arrays, places = (old.arrays, old.places) if isinstance(old, Spread) else (old, None)
    return pl.pallas_call(
        functools.partial(attend_kernel, old_places=places, first_key=first_key),
        out_shape=jax.ShapeDtypeStruct((rows, head_dim), jnp.bfloat16),
        in_specs=[SMEM] + [VMEM] * (2 + len(arrays)),
        out_specs=VMEM,
        scratch_shapes=[pltpu.VMEM((chips + 1, rows, rows), jnp.float32)],
        compiler_params=PARAMS,
        cost_estimate=pl.CostEstimate(
            flops=4 * rows * rows * chips * head_dim,
            bytes_accessed=4 * rows * chips * head_dim,
            transcendentals=rows * rows * chips,
        ),
    )(place, queries, fresh, *arrays)


def output_kernel(place_ref, attended_ref, act_ref, *refs, places, arrays):
    back_refs, refs = refs[:arrays], refs[arrays:]
    own_refs, other_refs, refs = refs[:NX], refs[NX : 2 * NX], refs[2 * NX :]
    half = attended_ref.shape[0] // 2
    back_ref = refs[0] if places else back_refs[0]
    if places:
        arrange(places, back_refs, back_ref, place_ref[0], place_ref[1])
    back_rows = back_ref.shape[1] * 3 // 4
    attended, activated = attended_ref[...], act_ref[...]
    dims = (((1,), (1,)), ((), ()))
    for k in range(NX):
        at = lax.rem(place_ref[2] + k, NX) * NY
        w_mlp = back_ref[pl.ds(at, NY), :back_rows, :].reshape(NY * back_rows, -1)
        w_att = jnp.concatenate([unpack(back_ref[at + j, back_rows:, :]) for j in range(NY)], 0)
        part = lax.dot_general(activated, w_mlp, dims, preferred_element_type=jnp.float32)
        part = part + lax.dot_general(
            attended, w_att, dims, preferred_element_type=jnp.float32
        )
        own_refs[k][...] = part[:half]
        other_refs[k][...] = part[half:].astype(jnp.bfloat16)


def output(place, attended, activated, back, width):
    rows = attended.shape[0]
    block = width // NX
    arrays, places, held = sources(back)
    kinds = [jnp.float32] * NX + [jnp.bfloat16] * NX
    outs = pl.pallas_call(
        functools.partial(output_kernel, places=places, arrays=len(arrays)),
        out_shape=[jax.ShapeDtypeStruct((rows // 2, block), kind) for kind in kinds] + held,
        in_specs=[SMEM] + [VMEM] * (2 + len(arrays)),
        out_specs=[VMEM] * (len(kinds) + len(held)),
        compiler_params=PARAMS,
        cost_estimate=pl.CostEstimate(
            flops=2 * rows * width * 512, bytes_accessed=2 * width * 512, transcendentals=0
        ),
    )(place, attended, activated, *arrays)
    return outs[:NX], outs[NX : 2 * NX], outs[2 * NX] if held else back


def layer_norm(current, mod_ref, entry):
    centred = current - jnp.mean(current, axis=-1, keepdims=True)
    variance = jnp.mean(centred * centred, axis=-1, keepdims=True)
    mod = mod_ref[entry]
    return (
        centred * lax.rsqrt(variance + epsilon) * (1.0 + mod[1:2, :]) + mod[0:1, :]
    ).astype(jnp.bfloat16)


def norm_kernel(times_ref, cur_ref, mod_ref, out_ref):
    out_ref[...] = layer_norm(cur_ref[...], mod_ref, times_ref[0])


def norm(timesteps, current, mod_table):
    rows, width = current.shape
    whole = pl.BlockSpec((rows // 3, width), lambda i: (i, 0))
    return pl.pallas_call(
        norm_kernel,
        out_shape=jax.ShapeDtypeStruct(current.shape, jnp.bfloat16),
        grid=(3,),
        in_specs=[SMEM, whole, pl.BlockSpec(mod_table.shape, lambda i: (0, 0, 0))],
        out_specs=whole,
        compiler_params=PARAMS,
        cost_estimate=pl.CostEstimate(
            flops=10 * current.size, bytes_accessed=6 * current.size, transcendentals=0
        ),
    )(timesteps, current, mod_table)


def update_kernel(place_ref, times_ref, sigma_ref, cur_ref, mod_ref, *refs, step):
    pieces, (out_a, out_b, branch_ref) = refs[:NX], refs[NX:]
    block = pieces[0].shape[1]
    for k in range(NX):
        at = pl.multiple_of(lax.rem(place_ref[2] + k, NX) * block, block)
        branch_ref[:, pl.ds(at, block)] = pieces[k][...].astype(jnp.float32)
    now, later = times_ref[step], times_ref[step + 1]
    current = cur_ref[...]
    velocity = current + mod_ref[now][2:3, :] * branch_ref[...]
    current = current + (sigma_ref[later] - sigma_ref[now]) * velocity
    if step + 1 == STEPS:
        out_a[...] = velocity
        out_b[...] = current
    else:
        out_a[...] = current
        out_b[...] = layer_norm(current, mod_ref, later)


def update(place, timesteps, sigmas, current, mod_table, pieces, step):
    rows, width = current.shape
    tile = rows // 3
    block = width // NX
    last = step + 1 == STEPS
    whole = pl.BlockSpec((tile, width), lambda i: (i, 0))
    return pl.pallas_call(
        functools.partial(update_kernel, step=step),
        out_shape=[
            jax.ShapeDtypeStruct(current.shape, jnp.float32),
            jax.ShapeDtypeStruct(current.shape, jnp.float32 if last else jnp.bfloat16),
        ],
        grid=(rows // tile,),
        in_specs=[SMEM] * 3
        + [whole, pl.BlockSpec(mod_table.shape, lambda i: (0, 0, 0))]
        + [pl.BlockSpec((tile, block), lambda i: (i, 0))] * NX,
        out_specs=[whole] * 2,
        scratch_shapes=[pltpu.VMEM((tile, width), jnp.float32)],
        compiler_params=PARAMS,
        cost_estimate=pl.CostEstimate(
            flops=20 * current.size, bytes_accessed=14 * current.size, transcendentals=0
        ),
    )(place, timesteps, sigmas, current, mod_table, *pieces)


def local(
    latent, timesteps, sigmas, mod_table, w_in, w_out, q_gain, k_gain, stale_keys, stale_values
):
    own_rows, width = latent.shape
    head_dim = q_gain.shape[0]
    patch = lax.axis_index("patch")
    c = patch % NC
    y = (patch // NC) % NY
    zl = patch // (NC * NY)
    x = lax.axis_index("tensor") % NX
    first = c == 0
    block = width // NY
    text_count = own_rows * lax.axis_size("patch") // 9

    def keep_and_send(for_core_0, for_core_1):
        return jnp.where(first, for_core_0, for_core_1), jnp.where(first, for_core_1, for_core_0)

    def in_core_order(keep, other):
        return jnp.where(
            first, jnp.concatenate([keep, other], 0), jnp.concatenate([other, keep], 0)
        )

    inner = 2 * head_dim
    hidden = (w_in.shape[1] - 3 * inner) // 2

    def qkv_columns(j):
        return jnp.concatenate(
            [w_in[:, i * inner + j * head_dim : i * inner + (j + 1) * head_dim] for i in range(3)], 1
        )

    def mlp_columns(j):
        return w_in[:, 3 * inner + j * hidden : 3 * inner + (j + 1) * hidden]

    def out_columns(j):
        return jnp.concatenate(
            [
                out_t[:, j * head_dim : (j + 1) * head_dim],
                out_t[:, inner + j * hidden : inner + (j + 1) * hidden],
            ],
            1,
        )

    def old_columns(j):
        return jnp.concatenate(
            [a[:, j * head_dim : (j + 1) * head_dim] for a in (stale_keys, stale_values)], 1
        )

    place = jnp.stack([zl, y, x])
    cat = functools.partial(jnp.concatenate, axis=0)

    keep, send = keep_and_send(qkv_columns(0), qkv_columns(1))
    other = swap_core(send)
    qkv_line = line_pieces(in_core_order(keep, other))
    keep, send = keep_and_send(old_columns(0), old_columns(1))
    old = cat([keep, swap_core(send)])
    old_values = after(old[:, head_dim:], qkv_line[1])
    old_values = [old_values] + [from_y(old_values, k) for k in range(1, NY)]
    w_in = after(w_in, old)
    keep, send = keep_and_send(mlp_columns(0), mlp_columns(1))
    mlp_block = cat([in_core_order(keep, swap_core(send)), pack(old[:, :head_dim])])

    qkv_message = cat(qkv_line)
    half = qkv_message.shape[0] // 2
    ahead_1, behind_1 = from_y(qkv_message, 1), from_y(qkv_message, NY - 1)
    mlp_line = line_pieces(after(mlp_block, (qkv_line, old_values)))
    w_out, patch, latent = after((w_out, patch, latent), mlp_line[1])
    first_normed = norm(timesteps, latent, mod_table)
    normed = first_normed, swap_core(first_normed)
    out_t = w_out.T
    back_rows = 2 * out_t.shape[0]
    cosine_table, sine_table = rope_tables(
        patch, patch + 1 - 2 * c, 2 * own_rows, head_dim, text_count
    )
    keep, send = keep_and_send(out_columns(0), out_columns(1))
    out_block = in_core_order(keep, swap_core(send))
    back_block = cat([out_block[:, head_dim:], pack(out_block[:, :head_dim])])

    mlp_message = cat(mlp_line)
    mlp_message, ahead_1, behind_1, back_block = after(
        (mlp_message, ahead_1, behind_1, back_block), normed
    )
    ahead_2, behind_2 = from_y(mlp_message, 1), from_y(mlp_message, NY - 1)
    near = from_z(back_block, 1)
    ahead_1h = from_y(after(ahead_1[half:], near), 1)
    behind_1h = from_y(after(behind_1[:half], near), NY - 1)
    far = from_z(after(back_block, near), 2)
    back_line = [back_block, near, far, from_z(after(back_block, far), 3)]

    back_message = cat(back_line)
    values_message = cat(old_values)
    back_message, values_message, ahead_2, behind_2 = after(
        (back_message, values_message, ahead_2, behind_2), (ahead_1h, behind_1h)
    )
    ahead_3, behind_3 = from_y(back_message, 1), from_y(back_message, NY - 1)
    half = mlp_message.shape[0] // 2
    near, last_piece = from_z(values_message, 1), from_z(values_message, 3)
    ahead_2h = from_y(ahead_2[half:], 1)
    far = from_z(after(values_message, near), 2)
    behind_2h = from_y(after(behind_2[:half], last_piece), NY - 1)
    old_values = [values_message, near, far, last_piece]
    w_qkv = Spread(qkv_line, (ahead_1, 0), (behind_1, 0), (ahead_1h, 0), (behind_1h, 0))
    w_mlp = Spread(mlp_line, (ahead_2, 0), (behind_2, 0), (ahead_2h, 0), (behind_2h, 0))

    def wave_4(fresh):
        ahead, behind = after((ahead_3, behind_3), (fresh, old_values, ahead_2h, behind_2h))
        half = back_message.shape[0] // 2
        ahead_3h = from_y(ahead[half:], 1)
        behind_3h = from_y(behind[:half], NY - 1)
        return Spread(back_line, (ahead, 0), (behind, 0), (ahead_3h, 0), (behind_3h, 0))

    current = latent

    for denoise in range(STEPS):
        last = denoise + 1 == STEPS
        queries, fresh, w_qkv = project_qkv(
            place, *normed, w_qkv, q_gain, k_gain, cosine_table, sine_table
        )
        if not last:
            w_back = wave_4(fresh)
        activated, w_mlp = project_mlp(place, *normed, w_mlp)
        old = old if last else [w_mlp] + old_values
        attended = attend(place, queries, fresh, old, back_rows)
        if not last:
            new_line = line_pieces(after(fresh, attended))
            new_message = cat(new_line)
            new_ahead, new_behind = from_y(new_message, 1), from_y(new_message, NY - 1)
        own, other, w_back = output(place, attended, activated, w_back, width)
        blocks = [
            (own[k] + swap_core(other[k]).astype(jnp.float32)).astype(jnp.bfloat16)
            for k in range(NX)
        ]
        total = blocks[0].astype(jnp.float32)
        for k in [2, 1, 3]:
            total = total + from_x(blocks[k], NX - k).astype(jnp.float32)
        half_sum = total.astype(jnp.bfloat16)
        total = half_sum.astype(jnp.float32) + swap_zh(half_sum).astype(jnp.float32)
        done = total.astype(jnp.bfloat16)
        if not last:
            done, new_ahead, new_behind = after((done, new_ahead, new_behind), done)
            half = new_message.shape[0] // 2
            new_halves = from_y(new_ahead[half:], 1), from_y(new_behind[:half], NY - 1)
            old = Spread(
                new_line,
                (new_ahead, 0),
                (new_behind, 0),
                (new_halves[0], 0),
                (new_halves[1], 0),
            )
        pieces = [done] + [from_x(done, k) for k in range(1, NX)]
        if not last:
            pieces = after(pieces, new_halves)
        new = update(place, timesteps, sigmas, current, mod_table, pieces, denoise)
        if last:
            return new
        current, normed = new
        normed = normed, swap_core(normed)


def solution(mesh):
    return jax.shard_map(
        local,
        mesh=mesh,
        in_specs=(
            P("patch", None),
            P(),
            P(),
            P(),
            P("patch", "tensor"),
            P("tensor", "patch"),
            P(),
            P(),
            P("patch", "tensor"),
            P("patch", "tensor"),
        ),
        out_specs=(P("patch", None), P("patch", None)),
        check_vma=False,
    )
```

```python
import functools

import jax
import numpy as np
import jax.numpy as jnp
from jax import lax
from jax.experimental import pallas as pl
from jax.experimental.pallas import tpu as pltpu
from jax.sharding import PartitionSpec as P

STEPS = 2
GRID = 64
epsilon = 1e-06

VMEM = pl.BlockSpec(memory_space=pltpu.VMEM)
SMEM = pl.BlockSpec(memory_space=pltpu.SMEM)
ANY = pl.BlockSpec(memory_space=pl.ANY)
PARAMS = pltpu.CompilerParams(vmem_limit_bytes=40 * 1024 * 1024)

NZ, NY, NC, NH, NX = 4, 4, 2, 2, 4
AXES = ("patch", "tensor")


def flat(zl, y, c, zh, x):
    return (((zl * NY + y) * NC + c) * NH + zh) * NX + x


def pairs(move):
    out = []
    for zl in range(NZ):
        for y in range(NY):
            for c in range(NC):
                for zh in range(NH):
                    for x in range(NX):
                        out.append((flat(zl, y, c, zh, x), flat(*move(zl, y, c, zh, x))))
    return out


def from_z(a, k):
    return lax.ppermute(a, AXES, pairs(lambda zl, y, c, zh, x: ((zl - k) % NZ, y, c, zh, x)))


def from_y(a, k):
    return lax.ppermute(a, AXES, pairs(lambda zl, y, c, zh, x: (zl, (y - k) % NY, c, zh, x)))


def swap_y(a):
    return lax.ppermute(a, AXES, pairs(lambda zl, y, c, zh, x: (zl, y ^ 1, c, zh, x)))


def flip_y(a):
    return lax.ppermute(a, AXES, pairs(lambda zl, y, c, zh, x: (zl, NY - 1 - y, c, zh, x)))


def from_x(a, k):
    return lax.ppermute(a, AXES, pairs(lambda zl, y, c, zh, x: (zl, y, c, zh, (x - k) % NX)))


def swap_core(a):
    return lax.ppermute(a, AXES, pairs(lambda zl, y, c, zh, x: (zl, y, 1 - c, zh, x)))


def swap_zh(a):
    return lax.ppermute(a, AXES, pairs(lambda zl, y, c, zh, x: (zl, y, c, 1 - zh, x)))


def frequencies(width_axis):
    return 1.0 / np.power(10000.0, np.arange(0, width_axis, 2) / width_axis)


def rope_rates(head_dim):
    first_width = head_dim // 8
    other_width = (head_dim - first_width) // 2
    none, rates = np.zeros(first_width // 2), frequencies(other_width)
    by_row = np.concatenate([none, rates, 0 * rates])
    by_column = np.concatenate([none, 0 * rates, rates])
    return np.repeat(np.stack([by_row, by_column]), 2, axis=1).astype(np.float32)


def rope_kernel(place_ref, rates_ref, cos_ref, sin_ref, *, text_count):
    rows, head_dim = cos_ref.shape
    half = rows // 2
    patch, other = place_ref[0], place_ref[1]
    index = lax.broadcasted_iota(jnp.int32, (rows, head_dim), 0)
    token = jnp.where(index < half, patch * half + index, other * half + index - half)
    image = jnp.maximum(token - text_count, 0)
    row = (image // GRID).astype(jnp.float32)
    column = (image % GRID).astype(jnp.float32)
    angles = row * rates_ref[0:1, :] + column * rates_ref[1:2, :]
    parity = lax.broadcasted_iota(jnp.int32, (rows, head_dim), 1) % 2
    cos_ref[...] = jnp.cos(angles)
    sin_ref[...] = jnp.sin(angles) * jnp.where(parity == 0, -1.0, 1.0)


def rope_tables(patch, other, rows, head_dim, text_count):
    return pl.pallas_call(
        functools.partial(rope_kernel, text_count=text_count),
        out_shape=[jax.ShapeDtypeStruct((rows, head_dim), jnp.float32)] * 2,
        in_specs=[SMEM, VMEM],
        out_specs=[VMEM] * 2,
        compiler_params=PARAMS,
    )(jnp.stack([patch, other]), jnp.asarray(rope_rates(head_dim)))


def after(array, done):
    return lax.optimization_barrier((array, done))[0]


def line_pieces(block):
    return [block] + [from_z(block, k) for k in range(1, NZ)]


def line_of(block):
    return jnp.concatenate(line_pieces(block), 0)


def pack(array):
    rows = array.shape[0] // 3
    return jnp.concatenate([array[i * rows : (i + 1) * rows] for i in range(3)], 1)


class Spread:
    def __init__(self, line, ahead, behind, ahead_half, behind_half):
        self.rows, self.columns = line[0].shape
        self.arrays = line + [s[0] for s in (ahead, behind, ahead_half, behind_half)]
        ahead, behind, ahead_half, behind_half = (
            s[1] for s in (ahead, behind, ahead_half, behind_half)
        )
        self.places = [(kz, 0, kz, 0) for kz in range(NZ)]
        self.places += [(NZ, ahead + kz * self.rows, kz, 1) for kz in range(NZ)]
        self.places += [(NZ + 1, behind + kz * self.rows, kz, NY - 1) for kz in range(NZ)]
        for kz in range(NZ):
            late = kz >= NZ // 2
            at = (ahead_half if late else behind_half) + kz % (NZ // 2) * self.rows
            self.places.append((NZ + 2 if late else NZ + 3, at, kz, 2))


def arrange(places, refs, held, zl, y):
    rows = held.shape[1]
    for n, at, kz, ky in places:
        chip = lax.rem(zl + kz, NZ) * NY + lax.rem(y + ky, NY)
        held[chip] = refs[n][at : at + rows, :]


def turn(columns, gain, cosine, sine):
    scaled = (
        columns
        * lax.rsqrt(jnp.mean(columns * columns, axis=-1, keepdims=True) + epsilon)
        * gain
    )
    width = columns.shape[1]
    parity = lax.broadcasted_iota(jnp.int32, columns.shape, 1) % 2
    swapped = jnp.where(
        parity == 0, pltpu.roll(scaled, width - 1, 1), pltpu.roll(scaled, 1, 1)
    )
    return (scaled * cosine + swapped * sine).astype(jnp.bfloat16)


def arranged(spread):
    return jax.ShapeDtypeStruct((NZ * NY, spread.rows, spread.columns), jnp.bfloat16)


def projected(places, place_ref, own_ref, other_ref, w_refs, held):
    if places is None:
        held = w_refs[0]
    else:
        arrange(places, w_refs, held, place_ref[0], place_ref[1])
    normed = jnp.concatenate([own_ref[...], other_ref[...]], 0)
    rows = normed.shape[1] // held.shape[0]
    w = held[:, :rows, :].reshape(normed.shape[1], held.shape[2])
    return jnp.dot(normed, w, preferred_element_type=jnp.float32)


def qkv_kernel(
    place_ref, own_ref, other_ref, qg_ref, kg_ref, cos_ref, sin_ref, *refs, places
):
    w_refs, held = (refs[:-2], None) if places is None else (refs[:-3], refs[-1])
    q_ref, fresh_ref = refs[len(w_refs) : len(w_refs) + 2]
    head_dim = q_ref.shape[1]
    qkv = projected(places, place_ref, own_ref, other_ref, w_refs, held)
    cosine, sine = cos_ref[...], sin_ref[...]
    q_ref[...] = turn(qkv[:, :head_dim], qg_ref[...], cosine, sine)
    fresh_ref[:, :head_dim] = turn(qkv[:, head_dim : 2 * head_dim], kg_ref[...], cosine, sine)
    fresh_ref[:, head_dim:] = qkv[:, 2 * head_dim :].astype(jnp.bfloat16)


def sources(w):
    if isinstance(w, Spread):
        return w.arrays, w.places, [arranged(w)]
    return [w], None, []


def project_cost(rows):
    size = 3072 * 384
    return pl.CostEstimate(flops=2 * rows * size, bytes_accessed=2 * size, transcendentals=0)


def project_qkv(place, own, other, w, q_gain, k_gain, cosine, sine):
    rows, head_dim = cosine.shape
    arrays, places, held = sources(w)
    outs = pl.pallas_call(
        functools.partial(qkv_kernel, places=places),
        out_shape=[
            jax.ShapeDtypeStruct((rows, head_dim), jnp.bfloat16),
            jax.ShapeDtypeStruct((rows, 2 * head_dim), jnp.bfloat16),
        ]
        + held,
        in_specs=[SMEM] + [VMEM] * (6 + len(arrays)),
        out_specs=[VMEM] * (2 + len(held)),
        compiler_params=PARAMS,
        cost_estimate=project_cost(rows),
    )(place, own, other, q_gain[None, :], k_gain[None, :], cosine, sine, *arrays)
    return outs[0], outs[1], outs[2] if held else w


def mlp_kernel(place_ref, own_ref, other_ref, *refs, places):
    w_refs, held = (refs[:-1], None) if places is None else (refs[:-2], refs[-1])
    hidden = projected(places, place_ref, own_ref, other_ref, w_refs, held)
    refs[len(w_refs)][...] = jax.nn.gelu(hidden, approximate=True).astype(jnp.bfloat16)


def project_mlp(place, own, other, w):
    rows = 2 * own.shape[0]
    arrays, places, held = sources(w)
    outs = pl.pallas_call(
        functools.partial(mlp_kernel, places=places),
        out_shape=[jax.ShapeDtypeStruct((rows, arrays[0].shape[-1]), jnp.bfloat16)] + held,
        in_specs=[SMEM] + [VMEM] * (2 + len(arrays)),
        out_specs=[VMEM] * (1 + len(held)),
        compiler_params=PARAMS,
        cost_estimate=project_cost(rows),
    )(place, own, other, *arrays)
    return outs[0], outs[1] if held else w


def unpack(packed):
    third = packed.shape[-1] // 3
    return jnp.concatenate([packed[:, i * third : (i + 1) * third] for i in range(3)], 0)


def attend_kernel(place_ref, q_ref, fresh_ref, *refs, old_places, first_key):
    old_refs, (out_ref, scores_ref) = refs[:-2], refs[-2:]
    rows, head_dim = q_ref.shape
    half = rows // 2
    zl, y = place_ref[0], place_ref[1]
    q = q_ref[...]
    scale = 1.0 / head_dim**0.5
    dims = (((1,), (1,)), ((), ()))
    row_patch = lax.broadcasted_iota(jnp.int32, (rows, rows), 0) // half
    col_patch = lax.broadcasted_iota(jnp.int32, (rows, rows), 1) // half
    same = row_patch == col_patch

    def old_keys(n):
        if old_places is None:
            chip = lax.rem(zl + n // NY, NZ) * NY + lax.rem(y + n % NY, NY)
            return unpack(old_refs[0][chip, first_key:, :])
        i, at, _, _ = old_places[n]
        return old_refs[i][at : at + rows, :head_dim]

    def old_values(n):
        if old_places is None:
            at = n % NY * rows
            return old_refs[1 + n // NY][at : at + rows, :]
        i, at, _, _ = old_places[n]
        return old_refs[i][at : at + rows, head_dim:]

    first = jnp.where(
        same,
        lax.dot_general(q, fresh_ref[:, :head_dim], dims, preferred_element_type=jnp.float32)
        * scale,
        -1e30,
    )
    scores_ref[0] = first
    top = jnp.max(first, axis=1, keepdims=True)
    chips = NZ * NY
    for n in range(chips):
        s = (
            lax.dot_general(q, old_keys(n), dims, preferred_element_type=jnp.float32)
            * scale
        )
        if n == 0:
            s = jnp.where(same, -1e30, s)
        scores_ref[n + 1] = s
        top = jnp.maximum(top, jnp.max(s, axis=1, keepdims=True))
    total = jnp.zeros((rows, 1), jnp.float32)
    mixed = jnp.zeros((rows, head_dim), jnp.float32)
    for n in range(chips + 1):
        e = jnp.exp(scores_ref[n] - top)
        total = total + jnp.sum(e, axis=1, keepdims=True)
        mixed = mixed + jnp.dot(
            e.astype(jnp.bfloat16),
            old_values(n - 1) if n else fresh_ref[:, head_dim:],
            preferred_element_type=jnp.float32,
        )
    out_ref[...] = (mixed / total).astype(jnp.bfloat16)


def attend(place, queries, fresh, old, first_key=0):
    rows, head_dim = queries.shape
    chips = NZ * NY
    arrays, places = (old.arrays, old.places) if isinstance(old, Spread) else (old, None)
    return pl.pallas_call(
        functools.partial(attend_kernel, old_places=places, first_key=first_key),
        out_shape=jax.ShapeDtypeStruct((rows, head_dim), jnp.bfloat16),
        in_specs=[SMEM] + [VMEM] * (2 + len(arrays)),
        out_specs=VMEM,
        scratch_shapes=[pltpu.VMEM((chips + 1, rows, rows), jnp.float32)],
        compiler_params=PARAMS,
        cost_estimate=pl.CostEstimate(
            flops=4 * rows * rows * chips * head_dim,
            bytes_accessed=4 * rows * chips * head_dim,
            transcendentals=rows * rows * chips,
        ),
    )(place, queries, fresh, *arrays)


def output_kernel(place_ref, attended_ref, act_ref, *refs, places, arrays):
    back_refs, refs = refs[:arrays], refs[arrays:]
    own_refs, other_refs, refs = refs[:NX], refs[NX : 2 * NX], refs[2 * NX :]
    half = attended_ref.shape[0] // 2
    back_ref = refs[0] if places else back_refs[0]
    if places:
        arrange(places, back_refs, back_ref, place_ref[0], place_ref[1])
    back_rows = back_ref.shape[1] * 3 // 4
    attended, activated = attended_ref[...], act_ref[...]
    dims = (((1,), (1,)), ((), ()))
    for k in range(NX):
        at = lax.rem(place_ref[2] + k, NX) * NY
        w_mlp = back_ref[pl.ds(at, NY), :back_rows, :].reshape(NY * back_rows, -1)
        w_att = jnp.concatenate([unpack(back_ref[at + j, back_rows:, :]) for j in range(NY)], 0)
        part = lax.dot_general(activated, w_mlp, dims, preferred_element_type=jnp.float32)
        part = part + lax.dot_general(
            attended, w_att, dims, preferred_element_type=jnp.float32
        )
        own_refs[k][...] = part[:half]
        other_refs[k][...] = part[half:].astype(jnp.bfloat16)


def output(place, attended, activated, back, width):
    rows = attended.shape[0]
    block = width // NX
    arrays, places, held = sources(back)
    kinds = [jnp.float32] * NX + [jnp.bfloat16] * NX
    outs = pl.pallas_call(
        functools.partial(output_kernel, places=places, arrays=len(arrays)),
        out_shape=[jax.ShapeDtypeStruct((rows // 2, block), kind) for kind in kinds] + held,
        in_specs=[SMEM] + [VMEM] * (2 + len(arrays)),
        out_specs=[VMEM] * (len(kinds) + len(held)),
        compiler_params=PARAMS,
        cost_estimate=pl.CostEstimate(
            flops=2 * rows * width * 512, bytes_accessed=2 * width * 512, transcendentals=0
        ),
    )(place, attended, activated, *arrays)
    return outs[:NX], outs[NX : 2 * NX], outs[2 * NX] if held else back


def layer_norm(current, mod_ref, entry):
    centred = current - jnp.mean(current, axis=-1, keepdims=True)
    variance = jnp.mean(centred * centred, axis=-1, keepdims=True)
    mod = mod_ref[entry]
    return (
        centred * lax.rsqrt(variance + epsilon) * (1.0 + mod[1:2, :]) + mod[0:1, :]
    ).astype(jnp.bfloat16)


def norm_kernel(times_ref, cur_ref, mod_ref, out_ref):
    out_ref[...] = layer_norm(cur_ref[...], mod_ref, times_ref[0])


def norm(timesteps, current, mod_table):
    rows, width = current.shape
    whole = pl.BlockSpec((rows // 3, width), lambda i: (i, 0))
    return pl.pallas_call(
        norm_kernel,
        out_shape=jax.ShapeDtypeStruct(current.shape, jnp.bfloat16),
        grid=(3,),
        in_specs=[SMEM, whole, pl.BlockSpec(mod_table.shape, lambda i: (0, 0, 0))],
        out_specs=whole,
        compiler_params=PARAMS,
        cost_estimate=pl.CostEstimate(
            flops=10 * current.size, bytes_accessed=6 * current.size, transcendentals=0
        ),
    )(timesteps, current, mod_table)


def update_kernel(place_ref, times_ref, sigma_ref, cur_ref, mod_ref, *refs, step):
    pieces, (out_a, out_b, branch_ref) = refs[:NX], refs[NX:]
    block = pieces[0].shape[1]
    for k in range(NX):
        at = pl.multiple_of(lax.rem(place_ref[2] + k, NX) * block, block)
        branch_ref[:, pl.ds(at, block)] = pieces[k][...].astype(jnp.float32)
    now, later = times_ref[step], times_ref[step + 1]
    current = cur_ref[...]
    velocity = current + mod_ref[now][2:3, :] * branch_ref[...]
    current = current + (sigma_ref[later] - sigma_ref[now]) * velocity
    if step + 1 == STEPS:
        out_a[...] = velocity
        out_b[...] = current
    else:
        out_a[...] = current
        out_b[...] = layer_norm(current, mod_ref, later)


def update(place, timesteps, sigmas, current, mod_table, pieces, step):
    rows, width = current.shape
    tile = rows // 3
    block = width // NX
    last = step + 1 == STEPS
    whole = pl.BlockSpec((tile, width), lambda i: (i, 0))
    return pl.pallas_call(
        functools.partial(update_kernel, step=step),
        out_shape=[
            jax.ShapeDtypeStruct(current.shape, jnp.float32),
            jax.ShapeDtypeStruct(current.shape, jnp.float32 if last else jnp.bfloat16),
        ],
        grid=(rows // tile,),
        in_specs=[SMEM] * 3
        + [whole, pl.BlockSpec(mod_table.shape, lambda i: (0, 0, 0))]
        + [pl.BlockSpec((tile, block), lambda i: (i, 0))] * NX,
        out_specs=[whole] * 2,
        scratch_shapes=[pltpu.VMEM((tile, width), jnp.float32)],
        compiler_params=PARAMS,
        cost_estimate=pl.CostEstimate(
            flops=20 * current.size, bytes_accessed=14 * current.size, transcendentals=0
        ),
    )(place, timesteps, sigmas, current, mod_table, *pieces)


def local(
    latent, timesteps, sigmas, mod_table, w_in, w_out, q_gain, k_gain, stale_keys, stale_values
):
    own_rows, width = latent.shape
    head_dim = q_gain.shape[0]
    patch = lax.axis_index("patch")
    c = patch % NC
    y = (patch // NC) % NY
    zl = patch // (NC * NY)
    x = lax.axis_index("tensor") % NX
    first = c == 0
    block = width // NY
    text_count = own_rows * lax.axis_size("patch") // 9

    def keep_and_send(for_core_0, for_core_1):
        return jnp.where(first, for_core_0, for_core_1), jnp.where(first, for_core_1, for_core_0)

    def in_core_order(keep, other):
        return jnp.where(
            first, jnp.concatenate([keep, other], 0), jnp.concatenate([other, keep], 0)
        )

    inner = 2 * head_dim
    hidden = (w_in.shape[1] - 3 * inner) // 2

    def qkv_columns(j):
        return jnp.concatenate(
            [w_in[:, i * inner + j * head_dim : i * inner + (j + 1) * head_dim] for i in range(3)], 1
        )

    def mlp_columns(j):
        return w_in[:, 3 * inner + j * hidden : 3 * inner + (j + 1) * hidden]

    def out_columns(j):
        return jnp.concatenate(
            [
                out_t[:, j * head_dim : (j + 1) * head_dim],
                out_t[:, inner + j * hidden : inner + (j + 1) * hidden],
            ],
            1,
        )

    def old_columns(j):
        return jnp.concatenate(
            [a[:, j * head_dim : (j + 1) * head_dim] for a in (stale_keys, stale_values)], 1
        )

    place = jnp.stack([zl, y, x])
    cat = functools.partial(jnp.concatenate, axis=0)

    keep, send = keep_and_send(qkv_columns(0), qkv_columns(1))
    other = swap_core(send)
    qkv_line = line_pieces(in_core_order(keep, other))
    keep, send = keep_and_send(old_columns(0), old_columns(1))
    old = cat([keep, swap_core(send)])
    old_values = after(old[:, head_dim:], qkv_line[1])
    old_values = [old_values] + [from_y(old_values, k) for k in range(1, NY)]
    w_in = after(w_in, old)
    keep, send = keep_and_send(mlp_columns(0), mlp_columns(1))
    mlp_block = cat([in_core_order(keep, swap_core(send)), pack(old[:, :head_dim])])

    qkv_message = cat(qkv_line)
    half = qkv_message.shape[0] // 2
    ahead_1, behind_1 = from_y(qkv_message, 1), from_y(qkv_message, NY - 1)
    mlp_line = line_pieces(after(mlp_block, (qkv_line, old_values)))
    w_out, patch, latent = after((w_out, patch, latent), mlp_line[1])
    first_normed = norm(timesteps, latent, mod_table)
    normed = first_normed, swap_core(first_normed)
    out_t = w_out.T
    back_rows = 2 * out_t.shape[0]
    cosine_table, sine_table = rope_tables(
        patch, patch + 1 - 2 * c, 2 * own_rows, head_dim, text_count
    )
    keep, send = keep_and_send(out_columns(0), out_columns(1))
    out_block = in_core_order(keep, swap_core(send))
    back_block = cat([out_block[:, head_dim:], pack(out_block[:, :head_dim])])

    mlp_message = cat(mlp_line)
    mlp_message, ahead_1, behind_1, back_block = after(
        (mlp_message, ahead_1, behind_1, back_block), normed
    )
    ahead_2, behind_2 = from_y(mlp_message, 1), from_y(mlp_message, NY - 1)
    near = from_z(back_block, 1)
    ahead_1h = from_y(after(ahead_1[half:], near), 1)
    behind_1h = from_y(after(behind_1[:half], near), NY - 1)
    far = from_z(after(back_block, near), 2)
    back_line = [back_block, near, far, from_z(after(back_block, far), 3)]

    back_message = cat(back_line)
    values_message = cat(old_values)
    back_message, values_message, ahead_2, behind_2 = after(
        (back_message, values_message, ahead_2, behind_2), (ahead_1h, behind_1h)
    )
    ahead_3, behind_3 = from_y(back_message, 1), from_y(back_message, NY - 1)
    half = mlp_message.shape[0] // 2
    near, last_piece = from_z(values_message, 1), from_z(values_message, 3)
    ahead_2h = from_y(ahead_2[half:], 1)
    far = from_z(after(values_message, near), 2)
    behind_2h = from_y(after(behind_2[:half], last_piece), NY - 1)
    old_values = [values_message, near, far, last_piece]
    w_qkv = Spread(qkv_line, (ahead_1, 0), (behind_1, 0), (ahead_1h, 0), (behind_1h, 0))
    w_mlp = Spread(mlp_line, (ahead_2, 0), (behind_2, 0), (ahead_2h, 0), (behind_2h, 0))

    def wave_4(fresh):
        ahead, behind = after((ahead_3, behind_3), (fresh, old_values, ahead_2h, behind_2h))
        half = back_message.shape[0] // 2
        ahead_3h = from_y(ahead[half:], 1)
        behind_3h = from_y(behind[:half], NY - 1)
        return Spread(back_line, (ahead, 0), (behind, 0), (ahead_3h, 0), (behind_3h, 0))

    current = latent

    for denoise in range(STEPS):
        last = denoise + 1 == STEPS
        queries, fresh, w_qkv = project_qkv(
            place, *normed, w_qkv, q_gain, k_gain, cosine_table, sine_table
        )
        if not last:
            w_back = wave_4(fresh)
        activated, w_mlp = project_mlp(place, *normed, w_mlp)
        old = old if last else [w_mlp] + old_values
        attended = attend(place, queries, fresh, old, back_rows)
        if not last:
            new_block = after(fresh, attended)
            near = from_z(new_block, 1)
            far = from_z(after(new_block, near), 2)
            new_line = [new_block, near, far, from_z(after(new_block, near), 3)]
            new_message = cat(new_line)
            new_ahead, new_behind = from_y(new_message, 1), from_y(new_message, NY - 1)
        own, other, w_back = output(place, attended, activated, w_back, width)
        blocks = [
            (own[k] + swap_core(other[k]).astype(jnp.float32)).astype(jnp.bfloat16)
            for k in range(NX)
        ]
        total = blocks[0].astype(jnp.float32)
        for k in [2, 1, 3]:
            total = total + from_x(blocks[k], NX - k).astype(jnp.float32)
        half_sum = total.astype(jnp.bfloat16)
        total = half_sum.astype(jnp.float32) + swap_zh(half_sum).astype(jnp.float32)
        done = total.astype(jnp.bfloat16)
        if not last:
            done, new_ahead, new_behind = after((done, new_ahead, new_behind), done)
            half = new_message.shape[0] // 2
            new_halves = from_y(new_ahead[half:], 1), from_y(new_behind[:half], NY - 1)
            old = Spread(
                new_line,
                (new_ahead, 0),
                (new_behind, 0),
                (new_halves[0], 0),
                (new_halves[1], 0),
            )
        pieces = [done] + [from_x(done, k) for k in range(1, NX)]
        if not last:
            pieces = after(pieces, new_halves)
        new = update(place, timesteps, sigmas, current, mod_table, pieces, denoise)
        if last:
            return new
        current, normed = new
        normed = normed, swap_core(normed)


def solution(mesh):
    return jax.shard_map(
        local,
        mesh=mesh,
        in_specs=(
            P("patch", None),
            P(),
            P(),
            P(),
            P("patch", "tensor"),
            P("tensor", "patch"),
            P(),
            P(),
            P("patch", "tensor"),
            P("patch", "tensor"),
        ),
        out_specs=(P("patch", None), P("patch", None)),
        check_vma=False,
    )
```
